32 devices in a mesh: dp: 8 (over z, core), ctx: 4 (over y, x).
Axes of the slice: x: 2, y: 2, z: 4, core: 2. Of those that a mesh axis runs over, the one named last changes fastest.
Arguments:
- queries: bfloat16 [8, 512, 2048], P('dp', 'ctx'), may hold values from -46 to 46
- keys_values: bfloat16 [8, 512, 1024], P('dp', 'ctx'), may hold values from -4 to 4
- grad_out: bfloat16 [8, 512, 4096], P('dp', 'ctx'), may hold values from -6 to 6
- out_proj: bfloat16 [2048, 4096], P('dp'), may hold values from -0.125 to 0.125
- doc_lengths: int32 [8, 16], P('dp'), may hold values from 1 to 64, as said below
- tile_mask: int32 [8, 4, 4], P('dp'), may hold values from 0 to 1, as said below
- unit_dest: int32 [8, 4, 2], P('dp'), may hold values from 0 to 3, as said below
Outputs:
- attn_out: bfloat16 [8, 512, 4096], P('dp', 'ctx')
- q_grad: bfloat16 [8, 512, 2048], P('dp', 'ctx')
- kv_grad: bfloat16 [8, 512, 1024], P('dp', 'ctx')
The draws below stay inside these ranges and needn't reach their ends.
Inputs may be any that keep to these rules, and one draw needn't show every extreme that they name: `doc_lengths`: each row sums to 512; exactly one entry equals 64. `tile_mask`: entry [b, a, c] is 1 exactly when some token of tile c precedes or equals some token of tile a in the same dialogue of doc_lengths[b]. Tokens j * 64 to (j + 1) * 64 - 1 of shard s become rows j * 64 to (j + 1) * 64 - 1 of shard unit_dest[b, s, j]; unit_dest[b, s, j] = (s + o_j) mod 4 with 2 distinct offsets o_j for each batch row.
All inputs are finite; a program needn't handle non-finite values.
Results may differ from the reference program's by a relative error of at most 0.012.
The reference program's roundings to bfloat16 on the way count: a program that leaves them out, or rounds other values in their place, can miss the bound.
Values may be sent and summed in bfloat16 or wider, within the bound.
No kernel may reach another device: no remote copies, remote signals or barrier semaphores. Data moves between devices by JAX's collectives and lax.ppermute only.
A program may use at most 128 MiB of HBM per device.

```python
import math
import jax
import jax.numpy as jnp
from jax import lax

D = 4096
QUERY_HEADS = 16
KEY_VALUE_HEADS = 4
HEAD_WIDTH = 128
TILE = 128
NDOC = 16
TOK_DEV = 128
PACKED_BATCH = 8
GROUPS = 4
SEQUENCE_TOKENS = 512
UNITS = 2
CAP = 64
NT = 4
LMAX = 64


def doc_layout(key):
    key = jax.random.fold_in(key, 11)
    row_keys = jax.random.split(key, PACKED_BATCH)

    def one_row(row_key):
        first_key, second_key = jax.random.split(row_key)
        base_len = (SEQUENCE_TOKENS - LMAX) // (NDOC - 1)
        leftover = SEQUENCE_TOKENS - LMAX - base_len * (NDOC - 1)
        extra = (jnp.arange(NDOC - 1) < leftover).astype(jnp.int32)
        jitter = jax.random.randint(first_key, (NDOC - 1,), 0, base_len)
        short_lengths = (base_len + extra + jitter - jnp.roll(jitter, -1)).astype(jnp.int32)
        all_lengths = jnp.concatenate([jnp.full((1,), LMAX, jnp.int32), short_lengths])
        return jnp.roll(all_lengths, jax.random.randint(second_key, (), 0, NDOC))
    return jax.vmap(one_row)(row_keys).astype(jnp.int32)


def draw_doc_lengths(key, part):
    return doc_layout(key)


def draw_tile_mask(key, part):
    lengths = doc_layout(key)
    ends = jnp.cumsum(lengths, axis=1)[:, :-1]
    tokens = jnp.arange(SEQUENCE_TOKENS, dtype=jnp.int32)
    docs = jnp.sum((tokens[None, :, None] >= ends[:, None, :]).astype(jnp.int32), axis=2)
    first_doc = docs[:, ::TILE]
    last_doc = docs[:, TILE - 1::TILE]
    tile_ids = jnp.arange(NT, dtype=jnp.int32)
    below = tile_ids[None, :] < tile_ids[:, None]
    reach = last_doc[:, None, :] >= first_doc[:, :, None]
    diagonal = tile_ids[None, :] == tile_ids[:, None]
    return (below[None] & reach | diagonal[None]).astype(jnp.int32)


def draw_unit_dest(key, part):
    key = jax.random.fold_in(key, 23)
    row_keys = jax.random.split(key, PACKED_BATCH)

    def row_routes(row_key):
        offsets = jax.random.permutation(row_key, GROUPS)[:UNITS]
        shard_ids = jnp.arange(GROUPS, dtype=jnp.int32)
        return (shard_ids[:, None] + offsets[None, :]) % GROUPS
    return jax.vmap(row_routes)(row_keys).astype(jnp.int32)


def shared_floats(key):
    key = jax.random.fold_in(key, 37)
    normal_key = jax.random.fold_in(key, 0)
    array_shape = (PACKED_BATCH, SEQUENCE_TOKENS, 2 * KEY_VALUE_HEADS * HEAD_WIDTH)
    base_values = jnp.clip(jax.random.normal(normal_key, array_shape, jnp.float32), -4.0, 4.0)
    return base_values


def draw_keys_values(key, part):
    base_values = shared_floats(key)
    return base_values.astype(jnp.bfloat16)


def draw_queries(key, part):
    key = jax.random.fold_in(key, 5)
    return jnp.clip(jax.random.normal(key, (PACKED_BATCH, SEQUENCE_TOKENS, QUERY_HEADS * HEAD_WIDTH), jnp.float32), -4.0, 4.0).astype(jnp.bfloat16)


def block_scale(stream_key, extent, pieces, least, high):
    gain, own = 1.0, jax.random.fold_in(stream_key, 6)
    for dim, parts in pieces:
        steps = jnp.exp(jax.random.uniform(jax.random.fold_in(own, dim), (parts,), jnp.float32, least / len(pieces), high / len(pieces)))
        gain = gain * jnp.repeat(steps, extent[dim] // parts).reshape([-1 if axis == dim else 1 for axis in range(len(extent))])
    return gain


def noise(own_key, dims, scale, bound, cuts=(), held_as=jnp.bfloat16):
    values = scale * jax.random.normal(own_key, dims, jnp.float32)
    if cuts:
        values = values * block_scale(own_key, dims, cuts, -0.22, 0.18)
    return jnp.clip(values, -bound, bound).astype(held_as)


def setup_inputs(seed: int = 0) -> dict:
    keys = jax.random.split(jax.random.key(seed), 8)
    return {
        "queries": draw_queries(jax.random.fold_in(keys[7], 71), 0),
        "keys_values": draw_keys_values(jax.random.fold_in(keys[7], 71), 0),
        "grad_out": noise(keys[2], (PACKED_BATCH, SEQUENCE_TOKENS, D), 1.0, 6.0, ((0, 8), (1, 4))),
        "out_proj": noise(keys[3], (QUERY_HEADS * HEAD_WIDTH, D), (QUERY_HEADS * HEAD_WIDTH) ** -0.5, 0.125, ((0, 8),)),
        "doc_lengths": draw_doc_lengths(jax.random.fold_in(keys[7], 71), 0),
        "tile_mask": draw_tile_mask(jax.random.fold_in(keys[7], 71), 0),
        "unit_dest": draw_unit_dest(jax.random.fold_in(keys[7], 71), 0),
    }


def unit_sources(routes):
    shard_ids = jnp.arange(routes.shape[0], dtype=jnp.int32)
    matches = (routes[:, None, :] == shard_ids[None, :, None]).astype(jnp.int32)
    return lax.optimization_barrier(jnp.sum(matches * shard_ids[:, None, None], axis=0))

def place_units(owners, per_shard, unit_rows):
    unit_count = owners.shape[1]
    starts = owners * per_shard + jnp.arange(unit_count, dtype=jnp.int32)[None, :] * unit_rows
    offsets = jnp.arange(unit_rows, dtype=jnp.int32)
    return (starts[:, :, None] + offsets[None, None, :]).reshape(-1).astype(jnp.int32)

def dialogue_of(positions, lengths):
    bounds = jnp.cumsum(lengths)[:-1]
    return lax.optimization_barrier(jnp.sum((positions[:, None] >= bounds[None, :]).astype(jnp.int32), axis=1))

def window_mask(query_pos, key_pos, lengths, tiles):
    query_doc = dialogue_of(query_pos.reshape(-1), lengths).reshape(query_pos.shape)
    key_doc = dialogue_of(key_pos.reshape(-1), lengths).reshape(key_pos.shape)
    tile_ids = jnp.arange(tiles.shape[0], dtype=jnp.int32)
    query_tiles = (query_pos[:, :, None] // TILE == tile_ids[None, None, :]).astype(jnp.float32)
    key_tiles = (key_pos[:, :, None] // TILE == tile_ids[None, None, :]).astype(jnp.float32)
    tile_rows = jnp.einsum('ucn,nm->ucm', query_tiles, tiles.astype(jnp.float32))
    tile_open = jnp.einsum('ucm,uwm->ucw', tile_rows, key_tiles) > 0.5
    same_doc = query_doc[:, :, None] == key_doc[:, None, :]
    causal = key_pos[:, None, :] <= query_pos[:, :, None]
    return tile_open & same_doc & causal

def shard_work(query_rows, grad_rows, query_pos, kv_row, lengths, tiles, out_proj):
    unit_count = query_pos.shape[0]
    width = LMAX + CAP
    scale = 1.0 / math.sqrt(HEAD_WIDTH)
    group_ratio = QUERY_HEADS // KEY_VALUE_HEADS
    key_head_width = KEY_VALUE_HEADS * HEAD_WIDTH
    win_start = jnp.clip(query_pos[:, 0] - LMAX, 0, SEQUENCE_TOKENS - width).astype(jnp.int32)
    key_pos = win_start[:, None] + jnp.arange(width, dtype=jnp.int32)[None, :]
    windows = jax.vmap(lambda start: lax.dynamic_slice_in_dim(kv_row, start, width, 0))(win_start).astype(jnp.float32)
    allowed = window_mask(query_pos, key_pos, lengths, tiles)
    q_units = query_rows.reshape(unit_count, CAP, QUERY_HEADS * HEAD_WIDTH).astype(jnp.float32)
    grad_context = jnp.dot(grad_rows, out_proj.T, preferred_element_type=jnp.float32).astype(jnp.bfloat16)

    def group_probs(query_head_group):
        q_part = q_units[:, :, query_head_group * group_ratio * HEAD_WIDTH:(query_head_group + 1) * group_ratio * HEAD_WIDTH].reshape(unit_count, CAP, group_ratio, HEAD_WIDTH)
        keys_part = windows[:, :, query_head_group * HEAD_WIDTH:(query_head_group + 1) * HEAD_WIDTH]
        raw = jnp.einsum('uchd,uwd->uhcw', q_part, keys_part) * scale
        masked = jnp.where(allowed[:, None], raw, -1e+30)
        top = lax.optimization_barrier(jnp.max(masked, axis=3, keepdims=True))
        expo = jnp.exp(masked - top)
        return (expo / lax.optimization_barrier(jnp.sum(expo, axis=3, keepdims=True)), q_part, keys_part)
    contexts = []
    for query_head_group in range(KEY_VALUE_HEADS):
        probs, q_part, keys_part = group_probs(query_head_group)
        values_part = windows[:, :, key_head_width + query_head_group * HEAD_WIDTH:key_head_width + (query_head_group + 1) * HEAD_WIDTH]
        weights = probs.astype(jnp.bfloat16).astype(jnp.float32)
        mixed = jnp.einsum('uhcw,uwd->uchd', weights, values_part).astype(jnp.bfloat16)
        contexts.append(mixed.reshape(unit_count * CAP, group_ratio * HEAD_WIDTH))
    context = jnp.concatenate(contexts, axis=1)
    attn_rows = jnp.dot(context, out_proj, preferred_element_type=jnp.float32).astype(jnp.bfloat16)
    delta = lax.optimization_barrier(jnp.sum(grad_context.astype(jnp.float32).reshape(-1, QUERY_HEADS, HEAD_WIDTH) * context.astype(jnp.float32).reshape(-1, QUERY_HEADS, HEAD_WIDTH), axis=2))
    delta_units = delta.reshape(unit_count, CAP, QUERY_HEADS)
    q_grads = []
    key_terms = []
    value_terms = []
    for query_head_group in range(KEY_VALUE_HEADS):
        probs, q_part, keys_part = group_probs(query_head_group)
        values_part = windows[:, :, key_head_width + query_head_group * HEAD_WIDTH:key_head_width + (query_head_group + 1) * HEAD_WIDTH]
        grad_part = grad_context[:, query_head_group * group_ratio * HEAD_WIDTH:(query_head_group + 1) * group_ratio * HEAD_WIDTH].astype(jnp.float32).reshape(unit_count, CAP, group_ratio, HEAD_WIDTH)
        delta_part = jnp.transpose(delta_units[:, :, query_head_group * group_ratio:(query_head_group + 1) * group_ratio], (0, 2, 1))
        grad_probs = jnp.einsum('uchd,uwd->uhcw', grad_part, values_part)
        grad_scores = (probs * (grad_probs - delta_part[:, :, :, None]) * scale).astype(jnp.bfloat16).astype(jnp.float32)
        q_grads.append(jnp.einsum('uhcw,uwd->uchd', grad_scores, keys_part).astype(jnp.bfloat16).reshape(unit_count * CAP, group_ratio * HEAD_WIDTH))
        key_terms.append(jnp.einsum('uhcw,uchd->uwd', grad_scores, q_part))
        value_terms.append(jnp.einsum('uhcw,uchd->uwd', probs.astype(jnp.bfloat16).astype(jnp.float32), grad_part))
    terms = jnp.concatenate(key_terms + value_terms, axis=2)

    def add_unit(index, total):
        start = win_start[index]
        current = lax.dynamic_slice_in_dim(total, start, width, 0)
        return lax.dynamic_update_slice_in_dim(total, current + terms[index], start, 0)
    placed = lax.fori_loop(0, unit_count, add_unit, jnp.zeros((SEQUENCE_TOKENS, 2 * key_head_width), jnp.float32))
    return (attn_rows, jnp.concatenate(q_grads, axis=1), placed)

def one_row(query_row, kv_row, grad_row, lengths, tiles, routes, out_proj):
    positions = place_units(unit_sources(routes), TOK_DEV, CAP)

    def shard_step(total, shard):
        query_pos = lax.dynamic_slice_in_dim(positions, shard * TOK_DEV, TOK_DEV).astype(jnp.int32)
        query_rows = query_row[query_pos]
        grad_rows = lax.dynamic_slice_in_dim(grad_row, shard * TOK_DEV, TOK_DEV, 0)
        attn_rows, q_rows, placed = shard_work(query_rows, grad_rows, query_pos.reshape(-1, CAP), kv_row, lengths, tiles, out_proj)
        rounded = lax.optimization_barrier(placed.astype(jnp.bfloat16)).astype(jnp.float32)
        return (total + rounded, (attn_rows, q_rows))
    starting_total = jnp.zeros((SEQUENCE_TOKENS, 2 * KEY_VALUE_HEADS * HEAD_WIDTH), jnp.float32)
    total, (attn_rows, q_rows) = lax.scan(shard_step, starting_total, jnp.arange(GROUPS, dtype=jnp.int32))
    kv_grad = total[positions].astype(jnp.bfloat16)
    return (attn_rows.reshape(SEQUENCE_TOKENS, -1), q_rows.reshape(SEQUENCE_TOKENS, -1), kv_grad)

def reference(queries, keys_values, grad_out, out_proj, doc_lengths, tile_mask, unit_dest):

    def per_batch(items):
        return one_row(items[0], items[1], items[2], items[3], items[4], items[5], out_proj)
    attn_out, q_grad, kv_grad = lax.map(per_batch, (queries, keys_values, grad_out, doc_lengths, tile_mask, unit_dest))
    return (attn_out, q_grad, kv_grad)
```

```python
import functools
import math

import jax
import jax.numpy as jnp
from jax import lax
from jax.experimental import pallas as pl
from jax.experimental.pallas import tpu as pltpu
from jax.sharding import PartitionSpec as P

QUERY_HEADS = 16
KEY_VALUE_HEADS = 4
HEAD_WIDTH = 128
TILE = 128
RATIO = QUERY_HEADS // KEY_VALUE_HEADS
GROUP_WIDTH = RATIO * HEAD_WIDTH
KEY_WIDTH = KEY_VALUE_HEADS * HEAD_WIDTH
SCALE = 1.0 / math.sqrt(HEAD_WIDTH)
F32 = jnp.float32
BF16 = jnp.bfloat16
NT_DIMS = (((1,), (1,)), ((), ()))
TN_DIMS = (((0,), (0,)), ((), ()))
VMEM_BYTES = 40 * 1024 * 1024


def whole():
    return pl.BlockSpec(memory_space=pltpu.VMEM)


def in_smem():
    return pl.BlockSpec(memory_space=pltpu.SMEM)


def anywhere():
    return pl.BlockSpec(memory_space=pl.ANY)


def dialogue_of(positions, lengths):
    bounds = jnp.cumsum(lengths)[:-1]
    return jnp.sum((positions[:, None] >= bounds[None, :]).astype(jnp.int32), axis=1)


def window_mask(query_pos, key_pos, lengths, tiles):
    query_doc = dialogue_of(query_pos.reshape(-1), lengths).reshape(query_pos.shape)
    key_doc = dialogue_of(key_pos.reshape(-1), lengths).reshape(key_pos.shape)
    tile_ids = jnp.arange(tiles.shape[0], dtype=jnp.int32)
    query_tiles = (query_pos[:, :, None] // TILE == tile_ids[None, None, :]).astype(F32)
    key_tiles = (key_pos[:, :, None] // TILE == tile_ids[None, None, :]).astype(F32)
    tile_rows = jnp.einsum("ucn,nm->ucm", query_tiles, tiles.astype(F32))
    tile_open = jnp.einsum("ucm,uwm->ucw", tile_rows, key_tiles) > 0.5
    same_doc = query_doc[:, :, None] == key_doc[:, None, :]
    causal = key_pos[:, None, :] <= query_pos[:, :, None]
    return tile_open & same_doc & causal


def stack_heads(block):
    return jnp.concatenate(
        [block[:, h * HEAD_WIDTH : (h + 1) * HEAD_WIDTH] for h in range(RATIO)], axis=0
    )


def forward_kernel(groups, units, rows, width, per_shard, *refs):
    meta, q_ref, allowed_ref = refs[:3]
    kv_parts = refs[3 : 3 + groups]
    context_ref, probs_ref, windows_ref = refs[3 + groups : 6 + groups]
    kv_ref, sems = refs[6 + groups :]
    me = meta[0]
    copies = []
    for t in range(groups):
        start = pl.multiple_of(jnp.bitwise_xor(me, t) * per_shard, per_shard)
        copies.append(
            pltpu.make_async_copy(kv_parts[t], kv_ref.at[pl.ds(start, per_shard)], sems.at[t])
        )
    for copy in copies:
        copy.start()
    for copy in copies:
        copy.wait()
    for u in range(units):
        start = pl.multiple_of(meta[3 + units + u], rows)
        window = kv_ref[pl.ds(start, width), :]
        windows_ref[u] = window
        mask = jnp.concatenate([allowed_ref[u]] * RATIO, axis=0) > 0.5
        for g in range(KEY_VALUE_HEADS):
            q_part = stack_heads(
                q_ref[u * rows : (u + 1) * rows, g * GROUP_WIDTH : (g + 1) * GROUP_WIDTH]
            )
            keys = window[:, g * HEAD_WIDTH : (g + 1) * HEAD_WIDTH]
            values = window[:, KEY_WIDTH + g * HEAD_WIDTH : KEY_WIDTH + (g + 1) * HEAD_WIDTH]
            raw = lax.dot_general(q_part, keys, NT_DIMS, preferred_element_type=F32) * SCALE
            masked = jnp.where(mask, raw, -1e30)
            top = jnp.max(masked, axis=1, keepdims=True)
            expo = jnp.exp(masked - top)
            probs = expo / jnp.sum(expo, axis=1, keepdims=True)
            probs_ref[g, u] = probs
            mixed = jnp.dot(probs.astype(BF16), values, preferred_element_type=F32).astype(BF16)
            for h in range(RATIO):
                col = (g * RATIO + h) * HEAD_WIDTH
                context_ref[u * rows : (u + 1) * rows, col : col + HEAD_WIDTH] = mixed[
                    h * rows : (h + 1) * rows
                ]


def group_of(meta, slot, swapped):
    return jnp.bitwise_xor(meta[1], slot) if swapped else slot


def grad_kernel(groups, units, rows, width, per_shard, slot, swapped, plan, with_q, *refs):
    meta, grad_ref, q_ref, context_ref, probs_ref, windows_ref = refs[:6]
    parts = refs[6 : 6 + len(plan)]
    rest = refs[6 + len(plan) :]
    if with_q:
        rest = rest[1:]
    q_grad_ref = rest[0]
    outs = rest[1 : 1 + groups]
    grad_context_ref, q_block, terms, sem = rest[1 + groups :]
    g = group_of(meta, slot, swapped)
    depth = parts[0].shape[0]
    sums = {}
    for part, (row_key, row_fn, col_fn) in zip(parts, plan):
        wide = part.shape[1]
        start = pl.multiple_of(col_fn(meta) * wide, wide)
        term = lax.dot_general(
            grad_ref[:, pl.ds(start, wide)], part[...], NT_DIMS, preferred_element_type=F32
        )
        sums[row_key] = (sums[row_key][0] + term if row_key in sums else term, row_fn)
    for total, row_fn in sums.values():
        grad_context_ref[row_fn(meta)] = total.astype(BF16)
    blocks = GROUP_WIDTH // depth
    grad_context = jnp.concatenate([grad_context_ref[b] for b in range(blocks)], axis=1)
    wide_start = pl.multiple_of(g * GROUP_WIDTH, GROUP_WIDTH)
    q_all = q_ref[:, pl.ds(wide_start, GROUP_WIDTH)]
    context_all = context_ref[:, pl.ds(wide_start, GROUP_WIDTH)]
    key_start = pl.multiple_of(g * HEAD_WIDTH, HEAD_WIDTH)
    value_start = pl.multiple_of(KEY_WIDTH + g * HEAD_WIDTH, HEAD_WIDTH)
    terms[...] = jnp.zeros_like(terms)
    for u in range(units):
        span = slice(u * rows, (u + 1) * rows)
        q_part = stack_heads(q_all[span])
        grad_part = stack_heads(grad_context[span])
        context_part = stack_heads(context_all[span])
        keys = windows_ref[u, :, pl.ds(key_start, HEAD_WIDTH)]
        values = windows_ref[u, :, pl.ds(value_start, HEAD_WIDTH)]
        probs = probs_ref[g, u]
        delta = jnp.sum(
            grad_part.astype(F32) * context_part.astype(F32), axis=1, keepdims=True
        )
        grad_probs = lax.dot_general(grad_part, values, NT_DIMS, preferred_element_type=F32)
        grad_scores = (probs * (grad_probs - delta) * SCALE).astype(BF16)
        q_part_grad = jnp.dot(grad_scores, keys, preferred_element_type=F32).astype(BF16)
        for h in range(RATIO):
            q_block[span, h * HEAD_WIDTH : (h + 1) * HEAD_WIDTH] = q_part_grad[
                h * rows : (h + 1) * rows
            ]
        key_term = lax.dot_general(grad_scores, q_part, TN_DIMS, preferred_element_type=F32)
        value_term = lax.dot_general(
            probs.astype(BF16), grad_part, TN_DIMS, preferred_element_type=F32
        )
        place = pl.ds(pl.multiple_of(meta[3 + units + u], rows), width)
        terms[place, :] += jnp.concatenate([key_term, value_term], axis=1)
    copy = pltpu.make_async_copy(q_block, q_grad_ref.at[:, pl.ds(wide_start, GROUP_WIDTH)], sem)
    copy.start()
    for t in range(groups):
        owner = jnp.bitwise_xor(meta[0], t)
        for u in range(units):
            shard = lax.rem(owner - meta[3 + u] + groups, groups)
            start = pl.multiple_of(shard * per_shard + u * rows, rows)
            outs[t][u * rows : (u + 1) * rows, :] = terms[pl.ds(start, rows), :].astype(BF16)
    copy.wait()


def project_kernel(slot, swapped, plan, first, meta, context_ref, *refs):
    parts = refs[: len(plan)]
    out_ref = refs[-1]
    total_ref = None if first else refs[len(plan)]
    g = group_of(meta, slot, swapped)
    by_columns = {}
    for part, (row_key, row_fn, col_fn) in zip(parts, plan):
        depth, wide = part.shape
        start = pl.multiple_of(g * GROUP_WIDTH + row_fn(meta) * depth, depth)
        term = jnp.dot(context_ref[:, pl.ds(start, depth)], part[...], preferred_element_type=F32)
        key = (id(col_fn), wide)
        if key in by_columns:
            by_columns[key] = (by_columns[key][0] + term, col_fn, wide)
        else:
            by_columns[key] = (term, col_fn, wide)
    for term, col_fn, wide in by_columns.values():
        span = pl.ds(pl.multiple_of(col_fn(meta) * wide, wide), wide)
        if not first:
            term = term + total_ref[:, span]
        out_ref[:, span] = term.astype(out_ref.dtype)


def combine_kernel(groups, order, swapped, meta, *refs):
    out_ref = refs[-1]
    for index, slot in enumerate(order):
        g = group_of(meta, slot, swapped)
        parts = refs[index * groups : (index + 1) * groups]
        total = parts[0][...].astype(F32)
        for part in parts[1:]:
            total = total + part[...].astype(F32)
        total = total.astype(BF16)
        out_ref[:, pl.ds(pl.multiple_of(g * HEAD_WIDTH, HEAD_WIDTH), HEAD_WIDTH)] = total[
            :, :HEAD_WIDTH
        ]
        out_ref[
            :, pl.ds(pl.multiple_of(KEY_WIDTH + g * HEAD_WIDTH, HEAD_WIDTH), HEAD_WIDTH)
        ] = total[:, HEAD_WIDTH:]


def zero_of(meta):
    return 0


def same_core(meta):
    return meta[2]


def other_core(meta):
    return 1 - meta[2]


def on_device(queries, keys_values, grad_out, out_proj, doc_lengths, tile_mask, unit_dest):
    groups = lax.axis_size("ctx")
    batches = lax.axis_size("dp")
    me = lax.axis_index("ctx").astype(jnp.int32)
    row = lax.axis_index("dp").astype(jnp.int32)
    per_shard = queries.shape[1]
    model = grad_out.shape[2]
    unit_count = unit_dest.shape[2]
    rows = per_shard // unit_count
    total_rows = per_shard * groups
    longest = total_rows // 8
    width = longest + rows
    lengths, tiles, routes = doc_lengths[0], tile_mask[0], unit_dest[0]
    offsets = routes[0]

    def move(block, fn):
        pairs = []
        for d in range(batches):
            for c in range(groups):
                d2, c2 = fn(d, c)
                pairs.append((d * groups + c, d2 * groups + c2))
        return lax.ppermute(block, ("dp", "ctx"), pairs)

    def to_ctx(block, t):
        return move(block, lambda d, c: (d, c ^ t))

    def to_core(block):
        return move(block, lambda d, c: (d ^ 1, c))

    def to_chip(block, j):
        return move(block, lambda d, c: (d ^ (2 * j), c))

    swapped = (batches // 2) * GROUP_WIDTH == QUERY_HEADS * HEAD_WIDTH and groups == 4
    slots = []
    if swapped:
        quarter = model // groups
        column_fns = [functools.partial(lambda t, meta: jnp.bitwise_xor(meta[0], t), t) for t in range(groups)]
        far = lax.dynamic_slice_in_dim(out_proj, me * quarter, quarter, 1)
        two = to_chip(far, 2)
        three = to_chip(two, 1)
        one = to_chip(out_proj, 1)
        for block in (out_proj, one):
            slots.append(
                [
                    (block, ("own", same_core, zero_of)),
                    (to_core(block), ("other", other_core, zero_of)),
                ]
            )
        for piece in (two, three):
            parts = []
            for t in range(groups):
                got = piece if t == 0 else to_ctx(piece, t)
                parts.append((got, ("own", same_core, column_fns[t])))
                parts.append((to_core(got), ("other", other_core, column_fns[t])))
            slots.append(parts)
    else:
        full = lax.all_gather(out_proj, "dp", axis=0, tiled=True)
        for g in range(KEY_VALUE_HEADS):
            part = full[g * GROUP_WIDTH : (g + 1) * GROUP_WIDTH]
            slots.append([(part, ("own", zero_of, zero_of))])

    q_units = queries[0].reshape(unit_count, rows, QUERY_HEADS * HEAD_WIDTH)
    dests = lax.rem(me + offsets, groups)
    sources = lax.rem(me - offsets + groups, groups)
    my_units = [q_units[j] for j in range(unit_count)]
    for t in range(1, groups):
        chosen = q_units[0]
        for j in range(1, unit_count):
            chosen = jnp.where(dests[j] == (me ^ t), q_units[j], chosen)
        got = to_ctx(chosen, t)
        my_units = [
            jnp.where(sources[j] == (me ^ t), got, my_units[j]) for j in range(unit_count)
        ]
    my_queries = jnp.concatenate(my_units, axis=0)
    kv_parts = [keys_values[0]] + [to_ctx(keys_values[0], t) for t in range(1, groups)]

    unit_ids = jnp.arange(unit_count, dtype=jnp.int32)
    first_pos = sources * per_shard + unit_ids * rows
    query_pos = first_pos[:, None] + jnp.arange(rows, dtype=jnp.int32)[None, :]
    win_start = jnp.clip(first_pos - longest, 0, total_rows - width)
    key_pos = win_start[:, None] + jnp.arange(width, dtype=jnp.int32)[None, :]
    allowed = window_mask(query_pos, key_pos, lengths, tiles).astype(F32)
    meta = jnp.concatenate(
        [jnp.stack([me, row // 2, lax.rem(row, 2)]), offsets, win_start]
    ).astype(jnp.int32)

    params = pltpu.CompilerParams(vmem_limit_bytes=VMEM_BYTES)
    sizes = (groups, unit_count, rows, width, per_shard)
    stacked = RATIO * rows
    context, probs, windows = pl.pallas_call(
        functools.partial(forward_kernel, *sizes),
        out_shape=(
            jax.ShapeDtypeStruct((per_shard, QUERY_HEADS * HEAD_WIDTH), BF16),
            jax.ShapeDtypeStruct((KEY_VALUE_HEADS, unit_count, stacked, width), F32),
            jax.ShapeDtypeStruct((unit_count, width, 2 * KEY_WIDTH), BF16),
        ),
        in_specs=[in_smem(), whole(), whole()] + [anywhere()] * groups,
        out_specs=(whole(), whole(), whole()),
        scratch_shapes=[
            pltpu.VMEM((total_rows, 2 * KEY_WIDTH), BF16),
            pltpu.SemaphoreType.DMA((groups,)),
        ],
        compiler_params=params,
        cost_estimate=pl.CostEstimate(
            flops=4 * unit_count * QUERY_HEADS * rows * width * HEAD_WIDTH * 8,
            bytes_accessed=8 * 1024 * 1024,
            transcendentals=unit_count * QUERY_HEADS * rows * width,
        ),
        name="forward",
    )(meta, my_queries, allowed, *kv_parts)

    q_grad = None
    total = None
    shares = []
    count = len(slots)
    for slot, parts in enumerate(slots):
        arrays = [part for part, _ in parts]
        plan = [entry for _, entry in parts]
        depth = arrays[0].shape[0]
        weight_bytes = GROUP_WIDTH * model * 2
        with_q = q_grad is not None
        results = pl.pallas_call(
            functools.partial(grad_kernel, *sizes, slot, swapped, plan, with_q),
            out_shape=(jax.ShapeDtypeStruct((per_shard, QUERY_HEADS * HEAD_WIDTH), BF16),)
            + tuple(
                jax.ShapeDtypeStruct((per_shard, 2 * HEAD_WIDTH), BF16) for _ in range(groups)
            ),
            in_specs=[in_smem()]
            + [whole()] * (5 + len(arrays))
            + ([anywhere()] if with_q else []),
            out_specs=(anywhere(),) + (whole(),) * groups,
            scratch_shapes=[
                pltpu.VMEM((GROUP_WIDTH // depth, per_shard, depth), BF16),
                pltpu.VMEM((per_shard, GROUP_WIDTH), BF16),
                pltpu.VMEM((total_rows, 2 * HEAD_WIDTH), F32),
                pltpu.SemaphoreType.DMA,
            ],
            input_output_aliases={6 + len(arrays): 0} if with_q else {},
            compiler_params=params,
            cost_estimate=pl.CostEstimate(
                flops=2 * per_shard * GROUP_WIDTH * model * 2,
                bytes_accessed=3 * weight_bytes,
                transcendentals=0,
            ),
            name=f"grad_{slot}",
        )(
            meta, grad_out[0], my_queries, context, probs, windows, *arrays,
            *([q_grad] if with_q else []),
        )
        q_grad = results[0]
        shares.append(
            [results[1]] + [to_ctx(results[1 + t], t) for t in range(1, groups)]
        )
        first = total is None
        last = slot == count - 1
        total = pl.pallas_call(
            functools.partial(project_kernel, slot, swapped, plan, first),
            out_shape=jax.ShapeDtypeStruct((per_shard, model), BF16 if last else F32),
            in_specs=[in_smem()] + [whole()] * (1 + len(arrays) + (0 if first else 1)),
            out_specs=whole(),
            compiler_params=params,
            cost_estimate=pl.CostEstimate(
                flops=2 * per_shard * GROUP_WIDTH * model,
                bytes_accessed=2 * weight_bytes,
                transcendentals=0,
            ),
            name=f"project_{slot}",
        )(meta, context, *arrays, *([] if first else [total]))

    kv_grad = pl.pallas_call(
        functools.partial(combine_kernel, groups, list(range(count)), swapped),
        out_shape=jax.ShapeDtypeStruct((per_shard, 2 * KEY_WIDTH), BF16),
        in_specs=[in_smem()] + [whole()] * (groups * count),
        out_specs=whole(),
        compiler_params=params,
        name="combine",
    )(meta, *[part for share in shares for part in share])
    return (total[None], q_grad[None], kv_grad[None])


def solution(mesh):
    return jax.shard_map(
        on_device,
        mesh=mesh,
        in_specs=(
            P("dp", "ctx", None),
            P("dp", "ctx", None),
            P("dp", "ctx", None),
            P("dp", None),
            P("dp", None),
            P("dp", None, None),
            P("dp", None, None),
        ),
        out_specs=(P("dp", "ctx", None), P("dp", "ctx", None), P("dp", "ctx", None)),
        check_vma=False,
    )
```

```python
import functools
import math

import jax
import jax.numpy as jnp
from jax import lax
from jax.experimental import pallas as pl
from jax.experimental.pallas import tpu as pltpu
from jax.sharding import PartitionSpec as P

QUERY_HEADS = 16
KEY_VALUE_HEADS = 4
HEAD_WIDTH = 128
TILE = 128
RATIO = QUERY_HEADS // KEY_VALUE_HEADS
GROUP_WIDTH = RATIO * HEAD_WIDTH
KEY_WIDTH = KEY_VALUE_HEADS * HEAD_WIDTH
SCALE = 1.0 / math.sqrt(HEAD_WIDTH)
F32 = jnp.float32
BF16 = jnp.bfloat16
NT_DIMS = (((1,), (1,)), ((), ()))
TN_DIMS = (((0,), (0,)), ((), ()))
VMEM_BYTES = 40 * 1024 * 1024


def whole():
    return pl.BlockSpec(memory_space=pltpu.VMEM)


def in_smem():
    return pl.BlockSpec(memory_space=pltpu.SMEM)


def anywhere():
    return pl.BlockSpec(memory_space=pl.ANY)


def dialogue_of(positions, lengths):
    bounds = jnp.cumsum(lengths)[:-1]
    return jnp.sum((positions[:, None] >= bounds[None, :]).astype(jnp.int32), axis=1)


def window_mask(query_pos, key_pos, lengths, tiles):
    query_doc = dialogue_of(query_pos.reshape(-1), lengths).reshape(query_pos.shape)
    key_doc = dialogue_of(key_pos.reshape(-1), lengths).reshape(key_pos.shape)
    tile_ids = jnp.arange(tiles.shape[0], dtype=jnp.int32)
    query_tiles = (query_pos[:, :, None] // TILE == tile_ids[None, None, :]).astype(F32)
    key_tiles = (key_pos[:, :, None] // TILE == tile_ids[None, None, :]).astype(F32)
    tile_rows = jnp.einsum("ucn,nm->ucm", query_tiles, tiles.astype(F32))
    tile_open = jnp.einsum("ucm,uwm->ucw", tile_rows, key_tiles) > 0.5
    same_doc = query_doc[:, :, None] == key_doc[:, None, :]
    causal = key_pos[:, None, :] <= query_pos[:, :, None]
    return tile_open & same_doc & causal


def stack_heads(block):
    return jnp.concatenate(
        [block[:, h * HEAD_WIDTH : (h + 1) * HEAD_WIDTH] for h in range(RATIO)], axis=0
    )


def forward_kernel(groups, units, rows, width, per_shard, *refs):
    meta, q_ref, allowed_ref = refs[:3]
    kv_parts = refs[3 : 3 + groups]
    context_ref, probs_ref, windows_ref = refs[3 + groups : 6 + groups]
    kv_ref, sems = refs[6 + groups :]
    me = meta[0]
    copies = []
    for t in range(groups):
        start = pl.multiple_of(jnp.bitwise_xor(me, t) * per_shard, per_shard)
        copies.append(
            pltpu.make_async_copy(
                kv_parts[t].at[pl.ds(0, per_shard)], kv_ref.at[pl.ds(start, per_shard)], sems.at[t])
        )
    for copy in copies:
        copy.start()
    for copy in copies:
        copy.wait()
    for u in range(units):
        start = pl.multiple_of(meta[3 + units + u], rows)
        window = kv_ref[pl.ds(start, width), :]
        windows_ref[u] = window
        mask = jnp.concatenate([allowed_ref[u]] * RATIO, axis=0) > 0.5
        for g in range(KEY_VALUE_HEADS):
            q_part = stack_heads(
                q_ref[u * rows : (u + 1) * rows, g * GROUP_WIDTH : (g + 1) * GROUP_WIDTH]
            )
            keys = window[:, g * HEAD_WIDTH : (g + 1) * HEAD_WIDTH]
            values = window[:, KEY_WIDTH + g * HEAD_WIDTH : KEY_WIDTH + (g + 1) * HEAD_WIDTH]
            raw = lax.dot_general(q_part, keys, NT_DIMS, preferred_element_type=F32) * SCALE
            masked = jnp.where(mask, raw, -1e30)
            top = jnp.max(masked, axis=1, keepdims=True)
            expo = jnp.exp(masked - top)
            probs = expo / jnp.sum(expo, axis=1, keepdims=True)
            probs_ref[g, u] = probs
            mixed = jnp.dot(probs.astype(BF16), values, preferred_element_type=F32).astype(BF16)
            for h in range(RATIO):
                col = (g * RATIO + h) * HEAD_WIDTH
                context_ref[u * rows : (u + 1) * rows, col : col + HEAD_WIDTH] = mixed[
                    h * rows : (h + 1) * rows
                ]


def group_of(meta, slot, swapped):
    return jnp.bitwise_xor(meta[1], slot) if swapped else slot


def grad_kernel(groups, units, rows, width, per_shard, slot, swapped, plan, with_q, *refs):
    meta, grad_ref, q_ref, context_ref, probs_ref, windows_ref = refs[:6]
    parts = refs[6 : 6 + len(plan)]
    rest = refs[6 + len(plan) :]
    if with_q:
        rest = rest[1:]
    q_grad_ref = rest[0]
    outs = rest[1 : 1 + groups]
    grad_context_ref, q_block, terms, sem = rest[1 + groups :]
    g = group_of(meta, slot, swapped)
    depth = parts[0].shape[0]
    sums = {}
    for part, (row_key, row_fn, col_fn) in zip(parts, plan):
        wide = part.shape[1]
        start = pl.multiple_of(col_fn(meta) * wide, wide)
        term = lax.dot_general(
            grad_ref[:, pl.ds(start, wide)], part[...], NT_DIMS, preferred_element_type=F32
        )
        sums[row_key] = (sums[row_key][0] + term if row_key in sums else term, row_fn)
    for total, row_fn in sums.values():
        grad_context_ref[row_fn(meta)] = total.astype(BF16)
    blocks = GROUP_WIDTH // depth
    grad_context = jnp.concatenate([grad_context_ref[b] for b in range(blocks)], axis=1)
    wide_start = pl.multiple_of(g * GROUP_WIDTH, GROUP_WIDTH)
    q_all = q_ref[:, pl.ds(wide_start, GROUP_WIDTH)]
    context_all = context_ref[:, pl.ds(wide_start, GROUP_WIDTH)]
    key_start = pl.multiple_of(g * HEAD_WIDTH, HEAD_WIDTH)
    value_start = pl.multiple_of(KEY_WIDTH + g * HEAD_WIDTH, HEAD_WIDTH)
    terms[...] = jnp.zeros_like(terms)
    for u in range(units):
        span = slice(u * rows, (u + 1) * rows)
        q_part = stack_heads(q_all[span])
        grad_part = stack_heads(grad_context[span])
        context_part = stack_heads(context_all[span])
        keys = windows_ref[u, :, pl.ds(key_start, HEAD_WIDTH)]
        values = windows_ref[u, :, pl.ds(value_start, HEAD_WIDTH)]
        probs = probs_ref[g, u]
        delta = jnp.sum(
            grad_part.astype(F32) * context_part.astype(F32), axis=1, keepdims=True
        )
        grad_probs = lax.dot_general(grad_part, values, NT_DIMS, preferred_element_type=F32)
        grad_scores = (probs * (grad_probs - delta) * SCALE).astype(BF16)
        q_part_grad = jnp.dot(grad_scores, keys, preferred_element_type=F32).astype(BF16)
        for h in range(RATIO):
            q_block[span, h * HEAD_WIDTH : (h + 1) * HEAD_WIDTH] = q_part_grad[
                h * rows : (h + 1) * rows
            ]
        key_term = lax.dot_general(grad_scores, q_part, TN_DIMS, preferred_element_type=F32)
        value_term = lax.dot_general(
            probs.astype(BF16), grad_part, TN_DIMS, preferred_element_type=F32
        )
        place = pl.ds(pl.multiple_of(meta[3 + units + u], rows), width)
        terms[place, :] += jnp.concatenate([key_term, value_term], axis=1)
    copy = pltpu.make_async_copy(q_block, q_grad_ref.at[:, pl.ds(wide_start, GROUP_WIDTH)], sem)
    copy.start()
    for t in range(groups):
        owner = jnp.bitwise_xor(meta[0], t)
        for u in range(units):
            shard = lax.rem(owner - meta[3 + u] + groups, groups)
            start = pl.multiple_of(shard * per_shard + u * rows, rows)
            outs[t][u * rows : (u + 1) * rows, :] = terms[pl.ds(start, rows), :].astype(BF16)
    copy.wait()


def project_kernel(slot, swapped, plan, first, meta, context_ref, *refs):
    parts = refs[: len(plan)]
    out_ref = refs[-1]
    total_ref = None if first else refs[len(plan)]
    g = group_of(meta, slot, swapped)
    by_columns = {}
    for part, (row_key, row_fn, col_fn) in zip(parts, plan):
        depth, wide = part.shape
        start = pl.multiple_of(g * GROUP_WIDTH + row_fn(meta) * depth, depth)
        term = jnp.dot(context_ref[:, pl.ds(start, depth)], part[...], preferred_element_type=F32)
        key = (id(col_fn), wide)
        if key in by_columns:
            by_columns[key] = (by_columns[key][0] + term, col_fn, wide)
        else:
            by_columns[key] = (term, col_fn, wide)
    for term, col_fn, wide in by_columns.values():
        span = pl.ds(pl.multiple_of(col_fn(meta) * wide, wide), wide)
        if not first:
            term = term + total_ref[:, span]
        out_ref[:, span] = term.astype(out_ref.dtype)


def combine_kernel(groups, order, swapped, meta, *refs):
    out_ref = refs[-1]
    for index, slot in enumerate(order):
        g = group_of(meta, slot, swapped)
        parts = refs[index * groups : (index + 1) * groups]
        total = parts[0][...].astype(F32)
        for part in parts[1:]:
            total = total + part[...].astype(F32)
        total = total.astype(BF16)
        out_ref[:, pl.ds(pl.multiple_of(g * HEAD_WIDTH, HEAD_WIDTH), HEAD_WIDTH)] = total[
            :, :HEAD_WIDTH
        ]
        out_ref[
            :, pl.ds(pl.multiple_of(KEY_WIDTH + g * HEAD_WIDTH, HEAD_WIDTH), HEAD_WIDTH)
        ] = total[:, HEAD_WIDTH:]


def zero_of(meta):
    return 0


def one_of(meta):
    return 1


def same_core(meta):
    return meta[2]


def other_core(meta):
    return 1 - meta[2]


def on_device(queries, keys_values, grad_out, out_proj, doc_lengths, tile_mask, unit_dest):
    groups = lax.axis_size("ctx")
    batches = lax.axis_size("dp")
    me = lax.axis_index("ctx").astype(jnp.int32)
    row = lax.axis_index("dp").astype(jnp.int32)
    per_shard = queries.shape[1]
    model = grad_out.shape[2]
    unit_count = unit_dest.shape[2]
    rows = per_shard // unit_count
    total_rows = per_shard * groups
    longest = total_rows // 8
    width = longest + rows
    lengths, tiles, routes = doc_lengths[0], tile_mask[0], unit_dest[0]
    offsets = routes[0]

    def move(block, fn):
        pairs = []
        for d in range(batches):
            for c in range(groups):
                d2, c2 = fn(d, c)
                pairs.append((d * groups + c, d2 * groups + c2))
        return lax.ppermute(block, ("dp", "ctx"), pairs)

    def to_ctx(block, t):
        return move(block, lambda d, c: (d, c ^ t))

    def to_core(block):
        return move(block, lambda d, c: (d ^ 1, c))

    def to_chip(block, j):
        return move(block, lambda d, c: (d ^ (2 * j), c))

    def after(block, *others):
        return lax.optimization_barrier((block,) + others)[0]

    swapped = (batches // 2) * GROUP_WIDTH == QUERY_HEADS * HEAD_WIDTH and groups == 4
    source = queries[0]
    if swapped:
        quarter = model // groups
        far = lax.dynamic_slice_in_dim(out_proj, me * quarter, quarter, 1)
        two = to_chip(far, 2)
        source = after(source, far)

    q_units = source.reshape(unit_count, rows, QUERY_HEADS * HEAD_WIDTH)
    dests = lax.rem(me + offsets, groups)
    sources = lax.rem(me - offsets + groups, groups)
    my_units = [q_units[j] for j in range(unit_count)]
    kv_parts = [keys_values[0]]
    kv_rows = keys_values.shape[1]
    for t in range(1, groups):
        chosen = q_units[0]
        for j in range(1, unit_count):
            chosen = jnp.where(dests[j] == (me ^ t), q_units[j], chosen)
        fold = QUERY_HEADS * HEAD_WIDTH // (2 * KEY_WIDTH)
        chosen = jnp.concatenate(
            [chosen[:, f * 2 * KEY_WIDTH : (f + 1) * 2 * KEY_WIDTH] for f in range(fold)], axis=0
        )
        sent = jnp.concatenate([keys_values[0], chosen], axis=0)
        if t == 1:
            first_sent = sent
        got = to_ctx(sent, t)
        kv_parts.append(got)
        got = jnp.concatenate(
            [got[kv_rows + f * rows : kv_rows + (f + 1) * rows] for f in range(fold)], axis=1
        )
        my_units = [
            jnp.where(sources[j] == (me ^ t), got, my_units[j]) for j in range(unit_count)
        ]
    my_queries = jnp.concatenate(my_units, axis=0)
    if swapped:
        half = model // 2
        one_a = to_chip(after(out_proj[:, :half], first_sent), 1)
        own_other = to_core(after(out_proj, kv_parts[1]))
        my_queries = after(my_queries, one_a)

    unit_ids = jnp.arange(unit_count, dtype=jnp.int32)
    first_pos = sources * per_shard + unit_ids * rows
    query_pos = first_pos[:, None] + jnp.arange(rows, dtype=jnp.int32)[None, :]
    win_start = jnp.clip(first_pos - longest, 0, total_rows - width)
    key_pos = win_start[:, None] + jnp.arange(width, dtype=jnp.int32)[None, :]
    allowed = window_mask(query_pos, key_pos, lengths, tiles).astype(F32)
    meta = jnp.concatenate(
        [jnp.stack([me, row // 2, lax.rem(row, 2)]), offsets, win_start]
    ).astype(jnp.int32)

    params = pltpu.CompilerParams(vmem_limit_bytes=VMEM_BYTES)
    sizes = (groups, unit_count, rows, width, per_shard)
    stacked = RATIO * rows
    context, probs, windows = pl.pallas_call(
        functools.partial(forward_kernel, *sizes),
        out_shape=(
            jax.ShapeDtypeStruct((per_shard, QUERY_HEADS * HEAD_WIDTH), BF16),
            jax.ShapeDtypeStruct((KEY_VALUE_HEADS, unit_count, stacked, width), F32),
            jax.ShapeDtypeStruct((unit_count, width, 2 * KEY_WIDTH), BF16),
        ),
        in_specs=[in_smem(), whole(), whole()] + [anywhere()] * groups,
        out_specs=(whole(), whole(), whole()),
        scratch_shapes=[
            pltpu.VMEM((total_rows, 2 * KEY_WIDTH), BF16),
            pltpu.SemaphoreType.DMA((groups,)),
        ],
        compiler_params=params,
        cost_estimate=pl.CostEstimate(
            flops=4 * unit_count * QUERY_HEADS * rows * width * HEAD_WIDTH * 8,
            bytes_accessed=8 * 1024 * 1024,
            transcendentals=unit_count * QUERY_HEADS * rows * width,
        ),
        name="forward",
    )(meta, my_queries, allowed, *kv_parts)

    q_grad = None
    total = None

    def grad_step(slot, parts, q_grad):
        arrays = [part for part, _ in parts]
        plan = [entry for _, entry in parts]
        depth = arrays[0].shape[0]
        with_q = q_grad is not None
        results = pl.pallas_call(
            functools.partial(grad_kernel, *sizes, slot, swapped, plan, with_q),
            out_shape=(jax.ShapeDtypeStruct((per_shard, QUERY_HEADS * HEAD_WIDTH), BF16),)
            + tuple(
                jax.ShapeDtypeStruct((per_shard, 2 * HEAD_WIDTH), BF16) for _ in range(groups)
            ),
            in_specs=[in_smem()]
            + [whole()] * (5 + len(arrays))
            + ([anywhere()] if with_q else []),
            out_specs=(anywhere(),) + (whole(),) * groups,
            scratch_shapes=[
                pltpu.VMEM((GROUP_WIDTH // depth, per_shard, depth), BF16),
                pltpu.VMEM((per_shard, GROUP_WIDTH), BF16),
                pltpu.VMEM((total_rows, 2 * HEAD_WIDTH), F32),
                pltpu.SemaphoreType.DMA,
            ],
            input_output_aliases={6 + len(arrays): 0} if with_q else {},
            compiler_params=params,
            cost_estimate=pl.CostEstimate(
                flops=2 * per_shard * GROUP_WIDTH * model * 2,
                bytes_accessed=3 * GROUP_WIDTH * model * 2,
                transcendentals=0,
            ),
            name=f"grad_{slot}",
        )(
            meta, grad_out[0], my_queries, context, probs, windows, *arrays,
            *([q_grad] if with_q else []),
        )
        return results[0], results[1:]

    def send_shares(mine):
        return [mine[0]] + [to_ctx(mine[t], t) for t in range(1, groups)]

    def project_step(slot, parts, total, last):
        arrays = [part for part, _ in parts]
        plan = [entry for _, entry in parts]
        first = total is None
        return pl.pallas_call(
            functools.partial(project_kernel, slot, swapped, plan, first),
            out_shape=jax.ShapeDtypeStruct((per_shard, model), BF16 if last else F32),
            in_specs=[in_smem()] + [whole()] * (1 + len(arrays) + (0 if first else 1)),
            out_specs=whole(),
            compiler_params=params,
            cost_estimate=pl.CostEstimate(
                flops=2 * per_shard * GROUP_WIDTH * model,
                bytes_accessed=2 * GROUP_WIDTH * model * 2,
                transcendentals=0,
            ),
            name=f"project_{slot}",
        )(meta, context, *arrays, *([] if first else [total]))

    shares = {}
    count = KEY_VALUE_HEADS
    if swapped:
        order = (0, 2, 1, 3)
        columns = [
            functools.partial(lambda t, meta: jnp.bitwise_xor(meta[0], t), t)
            for t in range(groups)
        ]

        def pair(block, column):
            return [
                (block, ("own", same_core, column)),
                (to_core(block), ("other", other_core, column)),
            ]

        parts_0 = [
            (out_proj, ("own", same_core, zero_of)),
            (own_other, ("other", other_core, zero_of)),
        ]
        three = to_chip(after(two, one_a, context, own_other), 1)
        q_grad, mine_0 = grad_step(0, parts_0, None)
        total = project_step(0, parts_0, None, False)
        twos = [two] + [to_ctx(after(two, *kv_parts[1:]), t) for t in range(1, groups)]
        one_b = to_chip(after(out_proj[:, half:], one_a, context), 1)
        middle = to_core(jnp.concatenate(twos + [one_a, three], axis=1))
        parts_2 = []
        for t in range(groups):
            parts_2.append((twos[t], ("own", same_core, columns[t])))
        for t in range(groups):
            parts_2.append(
                (middle[:, t * quarter : (t + 1) * quarter], ("other", other_core, columns[t]))
            )
        threes = [three] + [to_ctx(after(three, *twos[1:]), t) for t in range(1, groups)]
        parts_3 = [
            (three, ("own", same_core, columns[0])),
            (middle[:, model + half :], ("other", other_core, columns[0])),
        ]
        for t in range(1, groups):
            parts_3 += pair(threes[t], columns[t])
        q_grad, mine_2 = grad_step(2, parts_2, q_grad)
        total = project_step(2, parts_2, total, False)
        parts_1 = [
            (one_a, ("own", same_core, zero_of)),
            (middle[:, model : model + half], ("other", other_core, zero_of)),
        ]
        parts_1 += pair(after(one_b, total, mine_2[0], *threes[1:]), one_of)
        q_grad, mine_1 = grad_step(1, parts_1, q_grad)
        total = project_step(1, parts_1, total, False)
        merged = [
            jnp.concatenate([mine_0[t], mine_2[t], mine_1[t]], axis=1) for t in range(groups)
        ]
        early = send_shares(merged)
        for index, slot in enumerate((0, 2, 1)):
            span = slice(index * 2 * HEAD_WIDTH, (index + 1) * 2 * HEAD_WIDTH)
            shares[slot] = [part[:, span] for part in early]
        q_grad, mine_3 = grad_step(3, parts_3, q_grad)
        shares[3] = send_shares(mine_3)
        total = project_step(3, parts_3, total, True)
    else:
        full = lax.all_gather(out_proj, "dp", axis=0, tiled=True)
        for g in range(count):
            parts = [(full[g * GROUP_WIDTH : (g + 1) * GROUP_WIDTH], ("own", zero_of, zero_of))]
            q_grad, mine = grad_step(g, parts, q_grad)
            shares[g] = send_shares(mine)
            total = project_step(g, parts, total, g == count - 1)

    kv_grad = pl.pallas_call(
        functools.partial(combine_kernel, groups, list(range(count)), swapped),
        out_shape=jax.ShapeDtypeStruct((per_shard, 2 * KEY_WIDTH), BF16),
        in_specs=[in_smem()] + [whole()] * (groups * count),
        out_specs=whole(),
        compiler_params=params,
        name="combine",
    )(meta, *[part for slot in range(count) for part in shares[slot]])
    return (total[None], q_grad[None], kv_grad[None])


def solution(mesh):
    return jax.shard_map(
        on_device,
        mesh=mesh,
        in_specs=(
            P("dp", "ctx", None),
            P("dp", "ctx", None),
            P("dp", "ctx", None),
            P("dp", None),
            P("dp", None),
            P("dp", None, None),
            P("dp", None, None),
        ),
        out_specs=(P("dp", "ctx", None), P("dp", "ctx", None), P("dp", "ctx", None)),
        check_vma=False,
    )
```

```python
import functools
import math

import jax
import jax.numpy as jnp
from jax import lax
from jax.experimental import pallas as pl
from jax.experimental.pallas import tpu as pltpu
from jax.sharding import PartitionSpec as P

QUERY_HEADS = 16
KEY_VALUE_HEADS = 4
HEAD_WIDTH = 128
TILE = 128
RATIO = QUERY_HEADS // KEY_VALUE_HEADS
GROUP_WIDTH = RATIO * HEAD_WIDTH
KEY_WIDTH = KEY_VALUE_HEADS * HEAD_WIDTH
SCALE = 1.0 / math.sqrt(HEAD_WIDTH)
F32 = jnp.float32
BF16 = jnp.bfloat16
NT_DIMS = (((1,), (1,)), ((), ()))
TN_DIMS = (((0,), (0,)), ((), ()))
MIB = 1024 * 1024


def whole():
    return pl.BlockSpec(memory_space=pltpu.VMEM)


def in_smem():
    return pl.BlockSpec(memory_space=pltpu.SMEM)


def anywhere():
    return pl.BlockSpec(memory_space=pl.ANY)


def dialogue_of(positions, lengths):
    bounds = jnp.cumsum(lengths)[:-1]
    return jnp.sum((positions[:, None] >= bounds[None, :]).astype(jnp.int32), axis=1)


def window_mask(query_pos, key_pos, lengths, tiles):
    query_doc = dialogue_of(query_pos.reshape(-1), lengths).reshape(query_pos.shape)
    key_doc = dialogue_of(key_pos.reshape(-1), lengths).reshape(key_pos.shape)
    tile_ids = jnp.arange(tiles.shape[0], dtype=jnp.int32)
    query_tiles = (query_pos[:, :, None] // TILE == tile_ids[None, None, :]).astype(F32)
    key_tiles = (key_pos[:, :, None] // TILE == tile_ids[None, None, :]).astype(F32)
    tile_rows = jnp.einsum("ucn,nm->ucm", query_tiles, tiles.astype(F32))
    tile_open = jnp.einsum("ucm,uwm->ucw", tile_rows, key_tiles) > 0.5
    same_doc = query_doc[:, :, None] == key_doc[:, None, :]
    causal = key_pos[:, None, :] <= query_pos[:, :, None]
    return tile_open & same_doc & causal


def stack_heads(block):
    return jnp.concatenate(
        [block[:, h * HEAD_WIDTH : (h + 1) * HEAD_WIDTH] for h in range(RATIO)], axis=0
    )


def column_kernel(wide, meta, block_ref, out_ref, sem):
    start = pl.multiple_of(meta[0] * wide, wide)
    copy = pltpu.make_async_copy(block_ref.at[:, pl.ds(start, wide)], out_ref, sem)
    copy.start()
    copy.wait()


def pack_kernel(groups, units, rows, fold, meta, q_ref, kv_ref, *refs):
    outs, sems = refs[:-1], refs[-1]
    per_shard, wide = kv_ref.shape
    me = meta[0]
    copies = []
    for t in range(1, groups):
        chosen = 0
        for j in range(units):
            dest = lax.rem(me + meta[3 + j], groups)
            chosen = chosen + jnp.where(dest == jnp.bitwise_xor(me, t), j, 0)
        start = pl.multiple_of(chosen * rows, rows)
        copies.append((kv_ref, outs[t - 1].at[pl.ds(0, per_shard)]))
        for f in range(fold):
            copies.append(
                (
                    q_ref.at[pl.ds(start, rows), pl.ds(f * wide, wide)],
                    outs[t - 1].at[pl.ds(per_shard + f * rows, rows)],
                )
            )
    copies = [
        pltpu.make_async_copy(source, target, sems.at[i])
        for i, (source, target) in enumerate(copies)
    ]
    for copy in copies:
        copy.start()
    for copy in copies:
        copy.wait()


def forward_kernel(groups, units, rows, width, per_shard, fold, *refs):
    meta, allowed_ref, own_q = refs[:3]
    kv_parts = refs[3 : 3 + groups]
    context_ref, probs_ref, windows_ref, q_ref = refs[3 + groups : 7 + groups]
    kv_ref, kv_sems, q_sems = refs[7 + groups :]
    me = meta[0]
    wide = kv_ref.shape[1]
    for t in range(groups):
        start = pl.multiple_of(jnp.bitwise_xor(me, t) * per_shard, per_shard)
        pltpu.make_async_copy(
            kv_parts[t].at[pl.ds(0, per_shard)], kv_ref.at[pl.ds(start, per_shard)], kv_sems.at[t]
        ).start()
    for u in range(units):
        source = lax.rem(me - meta[3 + u] + groups, groups)
        for t in range(groups):

            @pl.when(source == jnp.bitwise_xor(me, t))
            def _():
                for f in range(fold):
                    if t == 0:
                        part = own_q.at[pl.ds(u * rows, rows), pl.ds(f * wide, wide)]
                    else:
                        part = kv_parts[t].at[pl.ds(per_shard + f * rows, rows)]
                    pltpu.make_async_copy(
                        part,
                        q_ref.at[pl.ds(u * rows, rows), pl.ds(f * wide, wide)],
                        q_sems.at[u, f],
                    ).start()

    for t in range(groups):
        start = pl.multiple_of(jnp.bitwise_xor(me, t) * per_shard, per_shard)
        pltpu.make_async_copy(
            kv_parts[t].at[pl.ds(0, per_shard)], kv_ref.at[pl.ds(start, per_shard)], kv_sems.at[t]
        ).wait()
    for u in range(units):
        for f in range(fold):
            pltpu.make_async_copy(
                own_q.at[pl.ds(u * rows, rows), pl.ds(f * wide, wide)],
                q_ref.at[pl.ds(u * rows, rows), pl.ds(f * wide, wide)],
                q_sems.at[u, f],
            ).wait()
    for u in range(units):
        start = pl.multiple_of(meta[3 + units + u], rows)
        window = kv_ref[pl.ds(start, width), :]
        windows_ref[u] = window
        mask = jnp.concatenate([allowed_ref[u]] * RATIO, axis=0) > 0.5
        for g in range(KEY_VALUE_HEADS):
            q_part = stack_heads(
                q_ref[u * rows : (u + 1) * rows, g * GROUP_WIDTH : (g + 1) * GROUP_WIDTH]
            )
            keys = window[:, g * HEAD_WIDTH : (g + 1) * HEAD_WIDTH]
            values = window[:, KEY_WIDTH + g * HEAD_WIDTH : KEY_WIDTH + (g + 1) * HEAD_WIDTH]
            raw = lax.dot_general(q_part, keys, NT_DIMS, preferred_element_type=F32) * SCALE
            masked = jnp.where(mask, raw, -1e30)
            top = jnp.max(masked, axis=1, keepdims=True)
            expo = jnp.exp(masked - top)
            probs = expo / jnp.sum(expo, axis=1, keepdims=True)
            probs_ref[g, u] = probs
            mixed = jnp.dot(probs.astype(BF16), values, preferred_element_type=F32).astype(BF16)
            for h in range(RATIO):
                col = (g * RATIO + h) * HEAD_WIDTH
                context_ref[u * rows : (u + 1) * rows, col : col + HEAD_WIDTH] = mixed[
                    h * rows : (h + 1) * rows
                ]


def group_of(meta, slot, swapped):
    return jnp.bitwise_xor(meta[1], slot) if swapped else slot


def grad_kernel(groups, units, rows, width, per_shard, slot, swapped, plan, with_q, stack, *refs):
    meta, grad_ref, q_ref, context_ref, probs_ref, windows_ref = refs[:6]
    count = 1 + max(entry[0] for entry in plan)
    parts = refs[6 : 6 + count]
    rest = refs[6 + count :]
    if with_q:
        rest = rest[1:]
    q_grad_ref = rest[0]
    outs = rest[1:-4]
    grad_context_ref, q_block, terms, sem = rest[-4:]
    g = group_of(meta, slot, swapped)
    depth = parts[0].shape[0]
    sums = {}
    for index, offset, wide, row_key, row_fn, col_fn in plan:
        start = pl.multiple_of(col_fn(meta) * wide, wide)
        term = lax.dot_general(
            grad_ref[:, pl.ds(start, wide)],
            parts[index][:, offset : offset + wide],
            NT_DIMS,
            preferred_element_type=F32,
        )
        sums[row_key] = (sums[row_key][0] + term if row_key in sums else term, row_fn)
    for total, row_fn in sums.values():
        grad_context_ref[row_fn(meta)] = total.astype(BF16)
    blocks = GROUP_WIDTH // depth
    grad_context = jnp.concatenate([grad_context_ref[b] for b in range(blocks)], axis=1)
    wide_start = pl.multiple_of(g * GROUP_WIDTH, GROUP_WIDTH)
    q_all = q_ref[:, pl.ds(wide_start, GROUP_WIDTH)]
    context_all = context_ref[:, pl.ds(wide_start, GROUP_WIDTH)]
    key_start = pl.multiple_of(g * HEAD_WIDTH, HEAD_WIDTH)
    value_start = pl.multiple_of(KEY_WIDTH + g * HEAD_WIDTH, HEAD_WIDTH)
    terms[...] = jnp.zeros_like(terms)
    for u in range(units):
        span = slice(u * rows, (u + 1) * rows)
        q_part = stack_heads(q_all[span])
        grad_part = stack_heads(grad_context[span])
        context_part = stack_heads(context_all[span])
        keys = windows_ref[u, :, pl.ds(key_start, HEAD_WIDTH)]
        values = windows_ref[u, :, pl.ds(value_start, HEAD_WIDTH)]
        probs = probs_ref[g, u]
        delta = jnp.sum(
            grad_part.astype(F32) * context_part.astype(F32), axis=1, keepdims=True
        )
        grad_probs = lax.dot_general(grad_part, values, NT_DIMS, preferred_element_type=F32)
        grad_scores = (probs * (grad_probs - delta) * SCALE).astype(BF16)
        q_part_grad = jnp.dot(grad_scores, keys, preferred_element_type=F32).astype(BF16)
        for h in range(RATIO):
            q_block[span, h * HEAD_WIDTH : (h + 1) * HEAD_WIDTH] = q_part_grad[
                h * rows : (h + 1) * rows
            ]
        key_term = lax.dot_general(grad_scores, q_part, TN_DIMS, preferred_element_type=F32)
        value_term = lax.dot_general(
            probs.astype(BF16), grad_part, TN_DIMS, preferred_element_type=F32
        )
        place = pl.ds(pl.multiple_of(meta[3 + units + u], rows), width)
        terms[place, :] += jnp.concatenate([key_term, value_term], axis=1)
    copy = pltpu.make_async_copy(q_block, q_grad_ref.at[:, pl.ds(wide_start, GROUP_WIDTH)], sem)
    copy.start()
    for t in range(groups):
        owner = jnp.bitwise_xor(meta[0], t)
        for u in range(units):
            shard = lax.rem(owner - meta[3 + u] + groups, groups)
            start = pl.multiple_of(shard * per_shard + u * rows, rows)
            share = terms[pl.ds(start, rows), :].astype(BF16)
            if stack:
                outs[0][owner, u * rows : (u + 1) * rows, :] = share
            else:
                outs[t][u * rows : (u + 1) * rows, :] = share
    copy.wait()


def project_kernel(slot, swapped, plan, first, meta, context_ref, *refs):
    count = 1 + max(entry[0] for entry in plan)
    parts = refs[:count]
    out_ref = refs[-1]
    total_ref = None if first else refs[count]
    g = group_of(meta, slot, swapped)
    by_columns = {}
    for index, offset, wide, row_key, row_fn, col_fn in plan:
        depth = parts[index].shape[0]
        start = pl.multiple_of(g * GROUP_WIDTH + row_fn(meta) * depth, depth)
        term = jnp.dot(
            context_ref[:, pl.ds(start, depth)],
            parts[index][:, offset : offset + wide],
            preferred_element_type=F32,
        )
        key = (id(col_fn), wide)
        if key in by_columns:
            by_columns[key] = (by_columns[key][0] + term, col_fn, wide)
        else:
            by_columns[key] = (term, col_fn, wide)
    for term, col_fn, wide in by_columns.values():
        span = pl.ds(pl.multiple_of(col_fn(meta) * wide, wide), wide)
        if not first:
            term = term + total_ref[:, span]
        out_ref[:, span] = term.astype(out_ref.dtype)


def combine_kernel(groups, order, swapped, with_out, meta, *refs):
    parts = refs[:groups]
    out_ref, sums, sems = refs[groups + with_out :]
    blocks = [part[...] for part in parts]
    if groups == 1:
        blocks = [parts[0][i] for i in range(parts[0].shape[0])]
    total = blocks[0].astype(F32)
    for block in blocks[1:]:
        total = total + block.astype(F32)
    sums[...] = total.astype(BF16)
    copies = []
    for index, slot in enumerate(order):
        g = group_of(meta, slot, swapped)
        for k in range(2):
            start = pl.multiple_of(k * KEY_WIDTH + g * HEAD_WIDTH, HEAD_WIDTH)
            copies.append(
                pltpu.make_async_copy(
                    sums.at[:, pl.ds((2 * index + k) * HEAD_WIDTH, HEAD_WIDTH)],
                    out_ref.at[:, pl.ds(start, HEAD_WIDTH)],
                    sems.at[2 * index + k],
                )
            )
    for copy in copies:
        copy.start()
    for copy in copies:
        copy.wait()


def zero_of(meta):
    return 0


def one_of(meta):
    return 1


def same_core(meta):
    return meta[2]


def other_core(meta):
    return 1 - meta[2]


def on_device(queries, keys_values, grad_out, out_proj, doc_lengths, tile_mask, unit_dest):
    groups = lax.axis_size("ctx")
    batches = lax.axis_size("dp")
    me = lax.axis_index("ctx").astype(jnp.int32)
    row = lax.axis_index("dp").astype(jnp.int32)
    per_shard = queries.shape[1]
    model = grad_out.shape[2]
    unit_count = unit_dest.shape[2]
    rows = per_shard // unit_count
    total_rows = per_shard * groups
    longest = total_rows // 8
    width = longest + rows
    lengths, tiles, routes = doc_lengths[0], tile_mask[0], unit_dest[0]
    offsets = routes[0]

    def move(block, fn):
        pairs = []
        for d in range(batches):
            for c in range(groups):
                d2, c2 = fn(d, c)
                pairs.append((d * groups + c, d2 * groups + c2))
        return lax.ppermute(block, ("dp", "ctx"), pairs)

    def to_ctx(block, t):
        return move(block, lambda d, c: (d, c ^ t))

    def to_core(block):
        return move(block, lambda d, c: (d ^ 1, c))

    def to_chip(block, j):
        return move(block, lambda d, c: (d ^ (2 * j), c))

    def after(block, *others):
        return lax.optimization_barrier((block,) + others)[0]

    swapped = (batches // 2) * GROUP_WIDTH == QUERY_HEADS * HEAD_WIDTH and groups == 4
    dests_meta = jnp.concatenate([jnp.stack([me, row // 2, lax.rem(row, 2)]), offsets])
    head_width = QUERY_HEADS * HEAD_WIDTH
    fold = head_width // (2 * KEY_WIDTH)
    sources = lax.rem(me - offsets + groups, groups)
    source = queries[0]
    if swapped:
        quarter = model // groups
        half = model // 2
        far = pl.pallas_call(
            functools.partial(column_kernel, quarter),
            out_shape=jax.ShapeDtypeStruct((out_proj.shape[0], quarter), BF16),
            in_specs=[in_smem(), anywhere()],
            out_specs=whole(),
            scratch_shapes=[pltpu.SemaphoreType.DMA],
            name="far",
        )(me[None], out_proj)
        two = to_chip(far, 2)
        source = after(source, far)
    sent = pl.pallas_call(
        functools.partial(pack_kernel, groups, unit_count, rows, fold),
        out_shape=tuple(
            jax.ShapeDtypeStruct((per_shard + fold * rows, 2 * KEY_WIDTH), BF16)
            for _ in range(1, groups)
        ),
        in_specs=[in_smem(), anywhere(), anywhere()],
        out_specs=(whole(),) * (groups - 1),
        scratch_shapes=[pltpu.SemaphoreType.DMA(((groups - 1) * (1 + fold),))],
        name="pack",
    )(dests_meta, source, keys_values[0])
    sent = list(sent)
    if swapped:
        own_other = to_core(out_proj)
        one_a = to_chip(after(out_proj[:, :half], own_other), 1)
        sent[-1] = after(sent[-1], own_other)
    kv_parts = [keys_values[0]] + [to_ctx(sent[t - 1], t) for t in range(1, groups)]

    unit_ids = jnp.arange(unit_count, dtype=jnp.int32)
    first_pos = sources * per_shard + unit_ids * rows
    query_pos = first_pos[:, None] + jnp.arange(rows, dtype=jnp.int32)[None, :]
    win_start = jnp.clip(first_pos - longest, 0, total_rows - width)
    key_pos = win_start[:, None] + jnp.arange(width, dtype=jnp.int32)[None, :]
    allowed = window_mask(query_pos, key_pos, lengths, tiles).astype(F32)
    meta = jnp.concatenate([dests_meta, win_start]).astype(jnp.int32)
    if swapped:
        allowed = after(allowed, one_a)

    params = pltpu.CompilerParams(vmem_limit_bytes=(16 if swapped else 40) * MIB)
    sizes = (groups, unit_count, rows, width, per_shard)
    stacked = RATIO * rows
    context, probs, windows, my_queries = pl.pallas_call(
        functools.partial(forward_kernel, *sizes, fold),
        out_shape=(
            jax.ShapeDtypeStruct((per_shard, QUERY_HEADS * HEAD_WIDTH), BF16),
            jax.ShapeDtypeStruct((KEY_VALUE_HEADS, unit_count, stacked, width), F32),
            jax.ShapeDtypeStruct((unit_count, width, 2 * KEY_WIDTH), BF16),
            jax.ShapeDtypeStruct((per_shard, head_width), BF16),
        ),
        in_specs=[in_smem(), whole(), anywhere()] + [anywhere()] * groups,
        out_specs=(whole(),) * 4,
        scratch_shapes=[
            pltpu.VMEM((total_rows, 2 * KEY_WIDTH), BF16),
            pltpu.SemaphoreType.DMA((groups,)),
            pltpu.SemaphoreType.DMA((unit_count, fold)),
        ],
        compiler_params=params,
        cost_estimate=pl.CostEstimate(
            flops=4 * unit_count * QUERY_HEADS * rows * width * HEAD_WIDTH * 8,
            bytes_accessed=8 * 1024 * 1024,
            transcendentals=unit_count * QUERY_HEADS * rows * width,
        ),
        name="forward",
    )(meta, allowed, queries[0], *kv_parts)

    q_grad = None
    total = None

    def arrange(parts):
        arrays, plan = [], []
        for block, offset, wide, *entry in parts:
            found = [i for i, array in enumerate(arrays) if array is block]
            if not found:
                arrays.append(block)
            plan.append((found[0] if found else len(arrays) - 1, offset, wide, *entry))
        return arrays, plan

    def grad_step(slot, parts, q_grad, stack=False):
        arrays, plan = arrange(parts)
        depth = arrays[0].shape[0]
        with_q = q_grad is not None
        results = pl.pallas_call(
            functools.partial(grad_kernel, *sizes, slot, swapped, plan, with_q, stack),
            out_shape=(jax.ShapeDtypeStruct((per_shard, QUERY_HEADS * HEAD_WIDTH), BF16),)
            + (
                (jax.ShapeDtypeStruct((groups, per_shard, 2 * HEAD_WIDTH), BF16),)
                if stack
                else (jax.ShapeDtypeStruct((per_shard, 2 * HEAD_WIDTH), BF16),) * groups
            ),
            in_specs=[in_smem()]
            + [whole()] * (5 + len(arrays))
            + ([anywhere()] if with_q else []),
            out_specs=(anywhere(),) + (whole(),) * (1 if stack else groups),
            scratch_shapes=[
                pltpu.VMEM((GROUP_WIDTH // depth, per_shard, depth), BF16),
                pltpu.VMEM((per_shard, GROUP_WIDTH), BF16),
                pltpu.VMEM((total_rows, 2 * HEAD_WIDTH), F32),
                pltpu.SemaphoreType.DMA,
            ],
            input_output_aliases={6 + len(arrays): 0} if with_q else {},
            compiler_params=params,
            cost_estimate=pl.CostEstimate(
                flops=2 * per_shard * GROUP_WIDTH * model * 2,
                bytes_accessed=3 * GROUP_WIDTH * model * 2,
                transcendentals=0,
            ),
            name=f"grad_{slot}",
        )(
            meta, grad_out[0], my_queries, context, probs, windows, *arrays,
            *([q_grad] if with_q else []),
        )
        return results[0], results[1:]

    def send_shares(mine):
        return [mine[0]] + [to_ctx(mine[t], t) for t in range(1, groups)]

    def project_step(slot, parts, total, last):
        arrays, plan = arrange(parts)
        first = total is None
        return pl.pallas_call(
            functools.partial(project_kernel, slot, swapped, plan, first),
            out_shape=jax.ShapeDtypeStruct((per_shard, model), BF16 if last else F32),
            in_specs=[in_smem()] + [whole()] * (1 + len(arrays) + (0 if first else 1)),
            out_specs=whole(),
            compiler_params=params,
            cost_estimate=pl.CostEstimate(
                flops=2 * per_shard * GROUP_WIDTH * model,
                bytes_accessed=2 * GROUP_WIDTH * model * 2,
                transcendentals=0,
            ),
            name=f"project_{slot}",
        )(meta, context, *arrays, *([] if first else [total]))

    count = KEY_VALUE_HEADS
    if swapped:
        order = (0, 2, 1, 3)
        columns = [
            functools.partial(lambda t, meta: jnp.bitwise_xor(meta[0], t), t)
            for t in range(groups)
        ]

        def own(block, column, offset=0, wide=None):
            return (block, offset, wide or block.shape[1], "own", same_core, column)

        def other(block, column, offset=0, wide=None):
            return (block, offset, wide or block.shape[1], "other", other_core, column)

        three = to_chip(two, 1)
        parts_0 = [own(out_proj, zero_of), other(own_other, zero_of)]
        q_grad, mine_0 = grad_step(0, parts_0, None)
        total = project_step(0, parts_0, None, False)
        twos = [two] + [to_ctx(after(two, *kv_parts[1:]), t) for t in range(1, groups)]
        one_b = to_chip(after(out_proj[:, half:], one_a), 1)
        middle = to_core(jnp.concatenate([one_a, three] + twos[:3] + [after(twos[3], total, mine_0[0])], axis=1))
        parts_2 = [own(twos[t], columns[t]) for t in range(groups)]
        parts_2 += [other(middle, columns[t], half + quarter + t * quarter, quarter) for t in range(groups)]
        threes = [three] + [to_ctx(after(three, *twos[1:]), t) for t in range(1, groups)]
        q_grad, mine_2 = grad_step(2, parts_2, q_grad)
        total = project_step(2, parts_2, total, False)
        one_b_other = to_core(after(one_b, total, mine_2[0], *threes[1:]))
        parts_1 = [
            own(one_a, zero_of),
            other(middle, zero_of, 0, half),
            own(one_b, one_of),
            other(one_b_other, one_of),
        ]
        parts_3 = [
            own(three, columns[0]),
            other(middle, columns[0], half, quarter),
        ]
        for t in range(1, groups):
            parts_3 += [own(threes[t], columns[t]), other(to_core(threes[t]), columns[t])]
        q_grad, mine_1 = grad_step(1, parts_1, q_grad)
        q_grad, mine_3 = grad_step(3, parts_3, q_grad)
        late = send_shares(
            [
                jnp.concatenate([mine_0[t], mine_2[t], mine_1[t], mine_3[t]], axis=1)
                for t in range(groups)
            ]
        )
        total = project_step(1, parts_1, total, False)
        total = project_step(3, parts_3, total, True)
        batches_of_shares = [((0, 2, 1, 3), late)]
    else:
        full = lax.all_gather(out_proj, "dp", axis=0, tiled=True)
        batches_of_shares = []
        for g in range(count):
            part = full[g * GROUP_WIDTH : (g + 1) * GROUP_WIDTH]
            parts = [(part, 0, model, "own", zero_of, zero_of)]
            q_grad, mine = grad_step(g, parts, q_grad)
            batches_of_shares.append(((g,), send_shares(mine)))
            total = project_step(g, parts, total, g == count - 1)

    kv_grad = None
    for order, share in batches_of_shares:
        with_out = kv_grad is not None
        kv_grad = pl.pallas_call(
            functools.partial(combine_kernel, len(share), order, swapped, int(with_out)),
            out_shape=jax.ShapeDtypeStruct((per_shard, 2 * KEY_WIDTH), BF16),
            in_specs=[in_smem()] + [whole()] * len(share) + [anywhere()] * int(with_out),
            out_specs=anywhere(),
            scratch_shapes=[
                pltpu.VMEM((per_shard, 2 * HEAD_WIDTH * len(order)), BF16),
                pltpu.SemaphoreType.DMA((2 * len(order),)),
            ],
            input_output_aliases={1 + len(share): 0} if with_out else {},
            compiler_params=params,
            name=f"combine_{order[0]}",
        )(meta, *share, *([kv_grad] if with_out else []))
    return (total[None], q_grad[None], kv_grad[None])


def solution(mesh):
    return jax.shard_map(
        on_device,
        mesh=mesh,
        in_specs=(
            P("dp", "ctx", None),
            P("dp", "ctx", None),
            P("dp", "ctx", None),
            P("dp", None),
            P("dp", None),
            P("dp", None, None),
            P("dp", None, None),
        ),
        out_specs=(P("dp", "ctx", None), P("dp", "ctx", None), P("dp", "ctx", None)),
        check_vma=False,
    )
```

```python
import functools
import math

import jax
import jax.numpy as jnp
from jax import lax
from jax.experimental import pallas as pl
from jax.experimental.pallas import tpu as pltpu
from jax.sharding import PartitionSpec as P

QUERY_HEADS = 16
KEY_VALUE_HEADS = 4
HEAD_WIDTH = 128
TILE = 128
RATIO = QUERY_HEADS // KEY_VALUE_HEADS
GROUP_WIDTH = RATIO * HEAD_WIDTH
KEY_WIDTH = KEY_VALUE_HEADS * HEAD_WIDTH
SCALE = 1.0 / math.sqrt(HEAD_WIDTH)
F32 = jnp.float32
BF16 = jnp.bfloat16
NT_DIMS = (((1,), (1,)), ((), ()))
TN_DIMS = (((0,), (0,)), ((), ()))
MIB = 1024 * 1024


def whole():
    return pl.BlockSpec(memory_space=pltpu.VMEM)


def in_smem():
    return pl.BlockSpec(memory_space=pltpu.SMEM)


def anywhere():
    return pl.BlockSpec(memory_space=pl.ANY)


def dialogue_of(positions, lengths):
    bounds = jnp.cumsum(lengths)[:-1]
    return jnp.sum((positions[:, None] >= bounds[None, :]).astype(jnp.int32), axis=1)


def window_mask(query_pos, key_pos, lengths, tiles):
    query_doc = dialogue_of(query_pos.reshape(-1), lengths).reshape(query_pos.shape)
    key_doc = dialogue_of(key_pos.reshape(-1), lengths).reshape(key_pos.shape)
    tile_ids = jnp.arange(tiles.shape[0], dtype=jnp.int32)
    query_tiles = (query_pos[:, :, None] // TILE == tile_ids[None, None, :]).astype(F32)
    key_tiles = (key_pos[:, :, None] // TILE == tile_ids[None, None, :]).astype(F32)
    tile_rows = jnp.einsum("ucn,nm->ucm", query_tiles, tiles.astype(F32))
    tile_open = jnp.einsum("ucm,uwm->ucw", tile_rows, key_tiles) > 0.5
    same_doc = query_doc[:, :, None] == key_doc[:, None, :]
    causal = key_pos[:, None, :] <= query_pos[:, :, None]
    return tile_open & same_doc & causal


def stack_heads(block):
    return jnp.concatenate(
        [block[:, h * HEAD_WIDTH : (h + 1) * HEAD_WIDTH] for h in range(RATIO)], axis=0
    )


def pack_kernel(groups, units, rows, fold, wide_far, routes, q_ref, kv_ref, *refs):
    outs, sems = refs[:-1], refs[-1]
    per_shard, wide = kv_ref.shape
    me = lax.axis_index("ctx")
    copies = []
    if wide_far:
        block_ref, outs = outs[0], outs[1:]
        start = pl.multiple_of(me * wide_far, wide_far)
        copies.append((block_ref.at[:, pl.ds(start, wide_far)], outs[-1]))
    for t in range(1, groups):
        chosen = 0
        for j in range(units):
            dest = lax.rem(me + routes[0, 0, j], groups)
            chosen = chosen + jnp.where(dest == jnp.bitwise_xor(me, t), j, 0)
        start = pl.multiple_of(chosen * rows, rows)
        copies.append((kv_ref, outs[t - 1].at[pl.ds(0, per_shard)]))
        for f in range(fold):
            copies.append(
                (
                    q_ref.at[pl.ds(start, rows), pl.ds(f * wide, wide)],
                    outs[t - 1].at[pl.ds(per_shard + f * rows, rows)],
                )
            )
    copies = [
        pltpu.make_async_copy(source, target, sems.at[i])
        for i, (source, target) in enumerate(copies)
    ]
    for copy in copies:
        copy.start()
    for copy in copies:
        copy.wait()


def forward_kernel(groups, units, rows, width, per_shard, fold, *refs):
    meta, allowed_ref, own_q = refs[:3]
    kv_parts = refs[3 : 3 + groups]
    context_ref, probs_ref, windows_ref, q_ref = refs[3 + groups : 7 + groups]
    kv_ref, kv_sems, q_sems = refs[7 + groups :]
    me = meta[0]
    wide = kv_ref.shape[1]
    for t in range(groups):
        start = pl.multiple_of(jnp.bitwise_xor(me, t) * per_shard, per_shard)
        pltpu.make_async_copy(
            kv_parts[t].at[pl.ds(0, per_shard)], kv_ref.at[pl.ds(start, per_shard)], kv_sems.at[t]
        ).start()
    for u in range(units):
        source = lax.rem(me - meta[3 + u] + groups, groups)
        for t in range(groups):

            @pl.when(source == jnp.bitwise_xor(me, t))
            def _():
                for f in range(fold):
                    if t == 0:
                        part = own_q.at[pl.ds(u * rows, rows), pl.ds(f * wide, wide)]
                    else:
                        part = kv_parts[t].at[pl.ds(per_shard + f * rows, rows)]
                    pltpu.make_async_copy(
                        part,
                        q_ref.at[pl.ds(u * rows, rows), pl.ds(f * wide, wide)],
                        q_sems.at[u, f],
                    ).start()

    for t in range(groups):
        start = pl.multiple_of(jnp.bitwise_xor(me, t) * per_shard, per_shard)
        pltpu.make_async_copy(
            kv_parts[t].at[pl.ds(0, per_shard)], kv_ref.at[pl.ds(start, per_shard)], kv_sems.at[t]
        ).wait()
    for u in range(units):
        for f in range(fold):
            pltpu.make_async_copy(
                own_q.at[pl.ds(u * rows, rows), pl.ds(f * wide, wide)],
                q_ref.at[pl.ds(u * rows, rows), pl.ds(f * wide, wide)],
                q_sems.at[u, f],
            ).wait()
    for u in range(units):
        start = pl.multiple_of(meta[3 + units + u], rows)
        window = kv_ref[pl.ds(start, width), :]
        windows_ref[u] = window
        mask = jnp.concatenate([allowed_ref[u]] * RATIO, axis=0) > 0.5
        for g in range(KEY_VALUE_HEADS):
            q_part = stack_heads(
                q_ref[u * rows : (u + 1) * rows, g * GROUP_WIDTH : (g + 1) * GROUP_WIDTH]
            )
            keys = window[:, g * HEAD_WIDTH : (g + 1) * HEAD_WIDTH]
            values = window[:, KEY_WIDTH + g * HEAD_WIDTH : KEY_WIDTH + (g + 1) * HEAD_WIDTH]
            raw = lax.dot_general(q_part, keys, NT_DIMS, preferred_element_type=F32) * SCALE
            masked = jnp.where(mask, raw, -1e30)
            top = jnp.max(masked, axis=1, keepdims=True)
            expo = jnp.exp(masked - top)
            probs = expo / jnp.sum(expo, axis=1, keepdims=True)
            probs_ref[g, u] = probs
            mixed = jnp.dot(probs.astype(BF16), values, preferred_element_type=F32).astype(BF16)
            for h in range(RATIO):
                col = (g * RATIO + h) * HEAD_WIDTH
                context_ref[u * rows : (u + 1) * rows, col : col + HEAD_WIDTH] = mixed[
                    h * rows : (h + 1) * rows
                ]


def group_of(meta, slot, swapped):
    return jnp.bitwise_xor(meta[1], slot) if swapped else slot


def grad_kernel(groups, units, rows, width, per_shard, slot, swapped, plan, with_q, stack, *refs):
    meta, grad_ref, q_ref, context_ref, probs_ref, windows_ref = refs[:6]
    count = 1 + max(entry[0] for entry in plan)
    parts = refs[6 : 6 + count]
    rest = refs[6 + count :]
    if with_q:
        rest = rest[1:]
    q_grad_ref = rest[0]
    outs = rest[1:-4]
    grad_context_ref, q_block, terms, sem = rest[-4:]
    g = group_of(meta, slot, swapped)
    depth = parts[0].shape[0]
    sums = {}
    for index, offset, wide, row_key, row_fn, col_fn in plan:
        start = pl.multiple_of(col_fn(meta) * wide, wide)
        term = lax.dot_general(
            grad_ref[:, pl.ds(start, wide)],
            parts[index][:, offset : offset + wide],
            NT_DIMS,
            preferred_element_type=F32,
        )
        sums[row_key] = (sums[row_key][0] + term if row_key in sums else term, row_fn)
    for total, row_fn in sums.values():
        grad_context_ref[row_fn(meta)] = total.astype(BF16)
    blocks = GROUP_WIDTH // depth
    grad_context = jnp.concatenate([grad_context_ref[b] for b in range(blocks)], axis=1)
    wide_start = pl.multiple_of(g * GROUP_WIDTH, GROUP_WIDTH)
    q_all = q_ref[:, pl.ds(wide_start, GROUP_WIDTH)]
    context_all = context_ref[:, pl.ds(wide_start, GROUP_WIDTH)]
    key_start = pl.multiple_of(g * HEAD_WIDTH, HEAD_WIDTH)
    value_start = pl.multiple_of(KEY_WIDTH + g * HEAD_WIDTH, HEAD_WIDTH)
    terms[...] = jnp.zeros_like(terms)
    for u in range(units):
        span = slice(u * rows, (u + 1) * rows)
        q_part = stack_heads(q_all[span])
        grad_part = stack_heads(grad_context[span])
        context_part = stack_heads(context_all[span])
        keys = windows_ref[u, :, pl.ds(key_start, HEAD_WIDTH)]
        values = windows_ref[u, :, pl.ds(value_start, HEAD_WIDTH)]
        probs = probs_ref[g, u]
        delta = jnp.sum(
            grad_part.astype(F32) * context_part.astype(F32), axis=1, keepdims=True
        )
        grad_probs = lax.dot_general(grad_part, values, NT_DIMS, preferred_element_type=F32)
        grad_scores = (probs * (grad_probs - delta) * SCALE).astype(BF16)
        q_part_grad = jnp.dot(grad_scores, keys, preferred_element_type=F32).astype(BF16)
        for h in range(RATIO):
            q_block[span, h * HEAD_WIDTH : (h + 1) * HEAD_WIDTH] = q_part_grad[
                h * rows : (h + 1) * rows
            ]
        key_term = lax.dot_general(grad_scores, q_part, TN_DIMS, preferred_element_type=F32)
        value_term = lax.dot_general(
            probs.astype(BF16), grad_part, TN_DIMS, preferred_element_type=F32
        )
        place = pl.ds(pl.multiple_of(meta[3 + units + u], rows), width)
        terms[place, :] += jnp.concatenate([key_term, value_term], axis=1)
    copy = pltpu.make_async_copy(q_block, q_grad_ref.at[:, pl.ds(wide_start, GROUP_WIDTH)], sem)
    copy.start()
    for t in range(groups):
        owner = jnp.bitwise_xor(meta[0], t)
        for u in range(units):
            shard = lax.rem(owner - meta[3 + u] + groups, groups)
            start = pl.multiple_of(shard * per_shard + u * rows, rows)
            share = terms[pl.ds(start, rows), :].astype(BF16)
            if stack:
                outs[0][owner, u * rows : (u + 1) * rows, :] = share
            else:
                outs[t][u * rows : (u + 1) * rows, :] = share
    copy.wait()


def project_kernel(slot, swapped, plan, first, meta, context_ref, *refs):
    count = 1 + max(entry[0] for entry in plan)
    parts = refs[:count]
    out_ref = refs[-1]
    total_ref = None if first else refs[count]
    g = group_of(meta, slot, swapped)
    by_columns = {}
    for index, offset, wide, row_key, row_fn, col_fn in plan:
        depth = parts[index].shape[0]
        start = pl.multiple_of(g * GROUP_WIDTH + row_fn(meta) * depth, depth)
        term = jnp.dot(
            context_ref[:, pl.ds(start, depth)],
            parts[index][:, offset : offset + wide],
            preferred_element_type=F32,
        )
        key = (id(col_fn), wide)
        if key in by_columns:
            by_columns[key] = (by_columns[key][0] + term, col_fn, wide)
        else:
            by_columns[key] = (term, col_fn, wide)
    for term, col_fn, wide in by_columns.values():
        span = pl.ds(pl.multiple_of(col_fn(meta) * wide, wide), wide)
        if not first:
            term = term + total_ref[:, span]
        out_ref[:, span] = term.astype(out_ref.dtype)


def combine_kernel(groups, order, swapped, with_out, meta, *refs):
    parts = refs[:groups]
    out_ref, sums, sems = refs[groups + with_out :]
    blocks = [part[...] for part in parts]
    if groups == 1:
        blocks = [parts[0][i] for i in range(parts[0].shape[0])]
    total = blocks[0].astype(F32)
    for block in blocks[1:]:
        total = total + block.astype(F32)
    sums[...] = total.astype(BF16)
    copies = []
    for index, slot in enumerate(order):
        g = group_of(meta, slot, swapped)
        for k in range(2):
            start = pl.multiple_of(k * KEY_WIDTH + g * HEAD_WIDTH, HEAD_WIDTH)
            copies.append(
                pltpu.make_async_copy(
                    sums.at[:, pl.ds((2 * index + k) * HEAD_WIDTH, HEAD_WIDTH)],
                    out_ref.at[:, pl.ds(start, HEAD_WIDTH)],
                    sems.at[2 * index + k],
                )
            )
    for copy in copies:
        copy.start()
    for copy in copies:
        copy.wait()


def zero_of(meta):
    return 0


def one_of(meta):
    return 1


def same_core(meta):
    return meta[2]


def other_core(meta):
    return 1 - meta[2]


def on_device(queries, keys_values, grad_out, out_proj, doc_lengths, tile_mask, unit_dest):
    groups = lax.axis_size("ctx")
    batches = lax.axis_size("dp")
    me = lax.axis_index("ctx").astype(jnp.int32)
    row = lax.axis_index("dp").astype(jnp.int32)
    per_shard = queries.shape[1]
    model = grad_out.shape[2]
    unit_count = unit_dest.shape[2]
    rows = per_shard // unit_count
    total_rows = per_shard * groups
    longest = total_rows // 8
    width = longest + rows
    lengths, tiles, routes = doc_lengths[0], tile_mask[0], unit_dest[0]
    offsets = routes[0]

    def move(block, fn):
        pairs = []
        for d in range(batches):
            for c in range(groups):
                d2, c2 = fn(d, c)
                pairs.append((d * groups + c, d2 * groups + c2))
        return lax.ppermute(block, ("dp", "ctx"), pairs)

    def to_ctx(block, t):
        return move(block, lambda d, c: (d, c ^ t))

    def to_core(block):
        return move(block, lambda d, c: (d ^ 1, c))

    def to_chip(block, j):
        return move(block, lambda d, c: (d ^ (2 * j), c))

    def after(block, *others):
        return lax.optimization_barrier((block,) + others)[0]

    swapped = (batches // 2) * GROUP_WIDTH == QUERY_HEADS * HEAD_WIDTH and groups == 4
    dests_meta = jnp.concatenate([jnp.stack([me, row // 2, lax.rem(row, 2)]), offsets])
    head_width = QUERY_HEADS * HEAD_WIDTH
    fold = head_width // (2 * KEY_WIDTH)
    sources = lax.rem(me - offsets + groups, groups)
    quarter = model // groups
    half = model // 2
    wide_far = quarter if swapped else 0
    shapes = [jax.ShapeDtypeStruct((per_shard + fold * rows, 2 * KEY_WIDTH), BF16)] * (groups - 1)
    if swapped:
        shapes.append(jax.ShapeDtypeStruct((out_proj.shape[0], quarter), BF16))
    sent = pl.pallas_call(
        functools.partial(pack_kernel, groups, unit_count, rows, fold, wide_far),
        out_shape=tuple(shapes),
        in_specs=[in_smem(), anywhere(), anywhere()] + [anywhere()] * int(swapped),
        out_specs=(whole(),) * len(shapes),
        scratch_shapes=[pltpu.SemaphoreType.DMA(((groups - 1) * (1 + fold) + int(swapped),))],
        name="pack",
    )(unit_dest, queries[0], keys_values[0], *([out_proj] if swapped else []))
    if swapped:
        two = to_chip(sent[-1], 2)
        sent = sent[:-1]
    sent = list(sent)
    if swapped:
        own_other = to_core(out_proj)
        one_a = to_chip(after(out_proj[:, :half], own_other), 1)
        sent[-1] = after(sent[-1], own_other)
    kv_parts = [keys_values[0]] + [to_ctx(sent[t - 1], t) for t in range(1, groups)]

    unit_ids = jnp.arange(unit_count, dtype=jnp.int32)
    first_pos = sources * per_shard + unit_ids * rows
    query_pos = first_pos[:, None] + jnp.arange(rows, dtype=jnp.int32)[None, :]
    win_start = jnp.clip(first_pos - longest, 0, total_rows - width)
    key_pos = win_start[:, None] + jnp.arange(width, dtype=jnp.int32)[None, :]
    allowed = window_mask(query_pos, key_pos, lengths, tiles).astype(F32)
    meta = jnp.concatenate([dests_meta, win_start]).astype(jnp.int32)

    params = pltpu.CompilerParams(vmem_limit_bytes=(16 if swapped else 40) * MIB)
    sizes = (groups, unit_count, rows, width, per_shard)
    stacked = RATIO * rows
    context, probs, windows, my_queries = pl.pallas_call(
        functools.partial(forward_kernel, *sizes, fold),
        out_shape=(
            jax.ShapeDtypeStruct((per_shard, QUERY_HEADS * HEAD_WIDTH), BF16),
            jax.ShapeDtypeStruct((KEY_VALUE_HEADS, unit_count, stacked, width), F32),
            jax.ShapeDtypeStruct((unit_count, width, 2 * KEY_WIDTH), BF16),
            jax.ShapeDtypeStruct((per_shard, head_width), BF16),
        ),
        in_specs=[in_smem(), whole(), anywhere()] + [anywhere()] * groups,
        out_specs=(whole(),) * 4,
        scratch_shapes=[
            pltpu.VMEM((total_rows, 2 * KEY_WIDTH), BF16),
            pltpu.SemaphoreType.DMA((groups,)),
            pltpu.SemaphoreType.DMA((unit_count, fold)),
        ],
        compiler_params=params,
        cost_estimate=pl.CostEstimate(
            flops=4 * unit_count * QUERY_HEADS * rows * width * HEAD_WIDTH * 8,
            bytes_accessed=8 * 1024 * 1024,
            transcendentals=unit_count * QUERY_HEADS * rows * width,
        ),
        name="forward",
    )(meta, allowed, queries[0], *kv_parts)

    q_grad = None
    total = None

    def arrange(parts):
        arrays, plan = [], []
        for block, offset, wide, *entry in parts:
            found = [i for i, array in enumerate(arrays) if array is block]
            if not found:
                arrays.append(block)
            plan.append((found[0] if found else len(arrays) - 1, offset, wide, *entry))
        return arrays, plan

    def grad_step(slot, parts, q_grad, stack=False):
        arrays, plan = arrange(parts)
        depth = arrays[0].shape[0]
        with_q = q_grad is not None
        results = pl.pallas_call(
            functools.partial(grad_kernel, *sizes, slot, swapped, plan, with_q, stack),
            out_shape=(jax.ShapeDtypeStruct((per_shard, QUERY_HEADS * HEAD_WIDTH), BF16),)
            + (
                (jax.ShapeDtypeStruct((groups, per_shard, 2 * HEAD_WIDTH), BF16),)
                if stack
                else (jax.ShapeDtypeStruct((per_shard, 2 * HEAD_WIDTH), BF16),) * groups
            ),
            in_specs=[in_smem()]
            + [whole()] * (5 + len(arrays))
            + ([anywhere()] if with_q else []),
            out_specs=(anywhere(),) + (whole(),) * (1 if stack else groups),
            scratch_shapes=[
                pltpu.VMEM((GROUP_WIDTH // depth, per_shard, depth), BF16),
                pltpu.VMEM((per_shard, GROUP_WIDTH), BF16),
                pltpu.VMEM((total_rows, 2 * HEAD_WIDTH), F32),
                pltpu.SemaphoreType.DMA,
            ],
            input_output_aliases={6 + len(arrays): 0} if with_q else {},
            compiler_params=params,
            cost_estimate=pl.CostEstimate(
                flops=2 * per_shard * GROUP_WIDTH * model * 2,
                bytes_accessed=3 * GROUP_WIDTH * model * 2,
                transcendentals=0,
            ),
            name=f"grad_{slot}",
        )(
            meta, grad_out[0], my_queries, context, probs, windows, *arrays,
            *([q_grad] if with_q else []),
        )
        return results[0], results[1:]

    def send_shares(mine):
        return [mine[0]] + [to_ctx(mine[t], t) for t in range(1, groups)]

    def project_step(slot, parts, total, last):
        arrays, plan = arrange(parts)
        first = total is None
        return pl.pallas_call(
            functools.partial(project_kernel, slot, swapped, plan, first),
            out_shape=jax.ShapeDtypeStruct((per_shard, model), BF16 if last else F32),
            in_specs=[in_smem()] + [whole()] * (1 + len(arrays) + (0 if first else 1)),
            out_specs=whole(),
            compiler_params=params,
            cost_estimate=pl.CostEstimate(
                flops=2 * per_shard * GROUP_WIDTH * model,
                bytes_accessed=2 * GROUP_WIDTH * model * 2,
                transcendentals=0,
            ),
            name=f"project_{slot}",
        )(meta, context, *arrays, *([] if first else [total]))

    count = KEY_VALUE_HEADS
    if swapped:
        order = (0, 2, 1, 3)
        columns = [
            functools.partial(lambda t, meta: jnp.bitwise_xor(meta[0], t), t)
            for t in range(groups)
        ]

        def own(block, column, offset=0, wide=None):
            return (block, offset, wide or block.shape[1], "own", same_core, column)

        def other(block, column, offset=0, wide=None):
            return (block, offset, wide or block.shape[1], "other", other_core, column)

        three = to_chip(two, 1)
        parts_0 = [own(out_proj, zero_of), other(own_other, zero_of)]
        q_grad, mine_0 = grad_step(0, parts_0, None)
        total = project_step(0, parts_0, None, False)
        twos = [two] + [to_ctx(after(two, *kv_parts[1:]), t) for t in range(1, groups)]
        one_b = to_chip(after(out_proj[:, half:], one_a), 1)
        middle = to_core(jnp.concatenate([one_a, three] + twos[:3] + [after(twos[3], total, mine_0[0])], axis=1))
        parts_2 = [own(twos[t], columns[t]) for t in range(groups)]
        parts_2 += [other(middle, columns[t], half + quarter + t * quarter, quarter) for t in range(groups)]
        threes = [three] + [to_ctx(after(three, *twos[1:]), t) for t in range(1, groups)]
        q_grad, mine_2 = grad_step(2, parts_2, q_grad)
        total = project_step(2, parts_2, total, False)
        one_b_other = to_core(after(one_b, total, mine_2[0], *threes[1:]))
        parts_1 = [
            own(one_a, zero_of),
            other(middle, zero_of, 0, half),
            own(one_b, one_of),
            other(one_b_other, one_of),
        ]
        parts_3 = [
            own(three, columns[0]),
            other(middle, columns[0], half, quarter),
        ]
        for t in range(1, groups):
            parts_3 += [own(threes[t], columns[t]), other(to_core(threes[t]), columns[t])]
        q_grad, mine_1 = grad_step(1, parts_1, q_grad)
        q_grad, mine_3 = grad_step(3, parts_3, q_grad)
        late = send_shares(
            [
                jnp.concatenate([mine_0[t], mine_2[t], mine_1[t], mine_3[t]], axis=1)
                for t in range(groups)
            ]
        )
        total = project_step(1, parts_1, total, False)
        total = project_step(3, parts_3, total, True)
        batches_of_shares = [((0, 2, 1, 3), late)]
    else:
        full = lax.all_gather(out_proj, "dp", axis=0, tiled=True)
        batches_of_shares = []
        for g in range(count):
            part = full[g * GROUP_WIDTH : (g + 1) * GROUP_WIDTH]
            parts = [(part, 0, model, "own", zero_of, zero_of)]
            q_grad, mine = grad_step(g, parts, q_grad)
            batches_of_shares.append(((g,), send_shares(mine)))
            total = project_step(g, parts, total, g == count - 1)

    kv_grad = None
    for order, share in batches_of_shares:
        with_out = kv_grad is not None
        kv_grad = pl.pallas_call(
            functools.partial(combine_kernel, len(share), order, swapped, int(with_out)),
            out_shape=jax.ShapeDtypeStruct((per_shard, 2 * KEY_WIDTH), BF16),
            in_specs=[in_smem()] + [whole()] * len(share) + [anywhere()] * int(with_out),
            out_specs=anywhere(),
            scratch_shapes=[
                pltpu.VMEM((per_shard, 2 * HEAD_WIDTH * len(order)), BF16),
                pltpu.SemaphoreType.DMA((2 * len(order),)),
            ],
            input_output_aliases={1 + len(share): 0} if with_out else {},
            compiler_params=params,
            name=f"combine_{order[0]}",
        )(meta, *share, *([kv_grad] if with_out else []))
    return (total[None], q_grad[None], kv_grad[None])


def solution(mesh):
    return jax.shard_map(
        on_device,
        mesh=mesh,
        in_specs=(
            P("dp", "ctx", None),
            P("dp", "ctx", None),
            P("dp", "ctx", None),
            P("dp", None),
            P("dp", None),
            P("dp", None, None),
            P("dp", None, None),
        ),
        out_specs=(P("dp", "ctx", None), P("dp", "ctx", None), P("dp", "ctx", None)),
        check_vma=False,
    )
```

```python
import functools
import math

import jax
import jax.numpy as jnp
from jax import lax
from jax.experimental import pallas as pl
from jax.experimental.pallas import tpu as pltpu
from jax.sharding import PartitionSpec as P

QUERY_HEADS = 16
KEY_VALUE_HEADS = 4
HEAD_WIDTH = 128
TILE = 128
RATIO = QUERY_HEADS // KEY_VALUE_HEADS
GROUP_WIDTH = RATIO * HEAD_WIDTH
KEY_WIDTH = KEY_VALUE_HEADS * HEAD_WIDTH
SCALE = 1.0 / math.sqrt(HEAD_WIDTH)
F32 = jnp.float32
BF16 = jnp.bfloat16
NT_DIMS = (((1,), (1,)), ((), ()))
TN_DIMS = (((0,), (0,)), ((), ()))
MIB = 1024 * 1024


def whole():
    return pl.BlockSpec(memory_space=pltpu.VMEM)


def in_smem():
    return pl.BlockSpec(memory_space=pltpu.SMEM)


def anywhere():
    return pl.BlockSpec(memory_space=pl.ANY)


def dialogue_of(positions, lengths):
    bounds = jnp.cumsum(lengths)[:-1]
    return jnp.sum((positions[:, None] >= bounds[None, :]).astype(jnp.int32), axis=1)


def window_mask(query_pos, key_pos, lengths, tiles):
    query_doc = dialogue_of(query_pos.reshape(-1), lengths).reshape(query_pos.shape)
    key_doc = dialogue_of(key_pos.reshape(-1), lengths).reshape(key_pos.shape)
    tile_ids = jnp.arange(tiles.shape[0], dtype=jnp.int32)
    query_tiles = (query_pos[:, :, None] // TILE == tile_ids[None, None, :]).astype(F32)
    key_tiles = (key_pos[:, :, None] // TILE == tile_ids[None, None, :]).astype(F32)
    tile_rows = jnp.einsum("ucn,nm->ucm", query_tiles, tiles.astype(F32))
    tile_open = jnp.einsum("ucm,uwm->ucw", tile_rows, key_tiles) > 0.5
    same_doc = query_doc[:, :, None] == key_doc[:, None, :]
    causal = key_pos[:, None, :] <= query_pos[:, :, None]
    return tile_open & same_doc & causal


def stack_heads(block):
    return jnp.concatenate(
        [block[:, h * HEAD_WIDTH : (h + 1) * HEAD_WIDTH] for h in range(RATIO)], axis=0
    )


def pack_kernel(groups, units, rows, fold, wide_far, routes, q_ref, kv_ref, *refs):
    outs, sems = refs[:-1], refs[-1]
    per_shard, wide = kv_ref.shape
    me = lax.axis_index("ctx")
    copies = []
    if wide_far:
        block_ref, outs = outs[0], outs[1:]
        start = pl.multiple_of(me * wide_far, wide_far)
        copies.append((block_ref.at[:, pl.ds(start, wide_far)], outs[-1]))
    for t in range(1, groups):
        chosen = 0
        for j in range(units):
            dest = lax.rem(me + routes[0, 0, j], groups)
            chosen = chosen + jnp.where(dest == jnp.bitwise_xor(me, t), j, 0)
        start = pl.multiple_of(chosen * rows, rows)
        copies.append((kv_ref, outs[t - 1].at[pl.ds(0, per_shard)]))
        for f in range(fold):
            copies.append(
                (
                    q_ref.at[pl.ds(start, rows), pl.ds(f * wide, wide)],
                    outs[t - 1].at[pl.ds(per_shard + f * rows, rows)],
                )
            )
    copies = [
        pltpu.make_async_copy(source, target, sems.at[i])
        for i, (source, target) in enumerate(copies)
    ]
    for copy in copies:
        copy.start()
    for copy in copies:
        copy.wait()


def forward_kernel(groups, units, rows, width, per_shard, fold, *refs):
    meta, allowed_ref, own_q = refs[:3]
    kv_parts = refs[3 : 3 + groups]
    context_ref, probs_ref, windows_ref, q_ref = refs[3 + groups : 7 + groups]
    kv_ref, kv_sems, q_sems = refs[7 + groups :]
    me = meta[0]
    wide = kv_ref.shape[1]
    for t in range(groups):
        start = pl.multiple_of(jnp.bitwise_xor(me, t) * per_shard, per_shard)
        pltpu.make_async_copy(
            kv_parts[t].at[pl.ds(0, per_shard)], kv_ref.at[pl.ds(start, per_shard)], kv_sems.at[t]
        ).start()
    for u in range(units):
        source = lax.rem(me - meta[3 + u] + groups, groups)
        for t in range(groups):

            @pl.when(source == jnp.bitwise_xor(me, t))
            def _():
                for f in range(fold):
                    if t == 0:
                        part = own_q.at[pl.ds(u * rows, rows), pl.ds(f * wide, wide)]
                    else:
                        part = kv_parts[t].at[pl.ds(per_shard + f * rows, rows)]
                    pltpu.make_async_copy(
                        part,
                        q_ref.at[pl.ds(u * rows, rows), pl.ds(f * wide, wide)],
                        q_sems.at[u, f],
                    ).start()

    for t in range(groups):
        start = pl.multiple_of(jnp.bitwise_xor(me, t) * per_shard, per_shard)
        pltpu.make_async_copy(
            kv_parts[t].at[pl.ds(0, per_shard)], kv_ref.at[pl.ds(start, per_shard)], kv_sems.at[t]
        ).wait()
    for u in range(units):
        for f in range(fold):
            pltpu.make_async_copy(
                own_q.at[pl.ds(u * rows, rows), pl.ds(f * wide, wide)],
                q_ref.at[pl.ds(u * rows, rows), pl.ds(f * wide, wide)],
                q_sems.at[u, f],
            ).wait()
    for u in range(units):
        start = pl.multiple_of(meta[3 + units + u], rows)
        window = kv_ref[pl.ds(start, width), :]
        windows_ref[u] = window
        mask = jnp.concatenate([allowed_ref[u]] * RATIO, axis=0) > 0.5
        for g in range(KEY_VALUE_HEADS):
            q_part = stack_heads(
                q_ref[u * rows : (u + 1) * rows, g * GROUP_WIDTH : (g + 1) * GROUP_WIDTH]
            )
            keys = window[:, g * HEAD_WIDTH : (g + 1) * HEAD_WIDTH]
            values = window[:, KEY_WIDTH + g * HEAD_WIDTH : KEY_WIDTH + (g + 1) * HEAD_WIDTH]
            raw = lax.dot_general(q_part, keys, NT_DIMS, preferred_element_type=F32) * SCALE
            masked = jnp.where(mask, raw, -1e30)
            top = jnp.max(masked, axis=1, keepdims=True)
            expo = jnp.exp(masked - top)
            probs = expo / jnp.sum(expo, axis=1, keepdims=True)
            probs_ref[g, u] = probs
            mixed = jnp.dot(probs.astype(BF16), values, preferred_element_type=F32).astype(BF16)
            for h in range(RATIO):
                col = (g * RATIO + h) * HEAD_WIDTH
                context_ref[u * rows : (u + 1) * rows, col : col + HEAD_WIDTH] = mixed[
                    h * rows : (h + 1) * rows
                ]


def group_of(meta, slot, swapped):
    return jnp.bitwise_xor(meta[1], slot) if swapped else slot


def grad_kernel(groups, units, rows, width, per_shard, slot, swapped, plan, with_q, stack, *refs):
    meta, grad_ref, q_ref, context_ref, probs_ref, windows_ref = refs[:6]
    count = 1 + max(entry[0] for entry in plan)
    parts = refs[6 : 6 + count]
    rest = refs[6 + count :]
    if with_q:
        rest = rest[1:]
    q_grad_ref = rest[0]
    outs = rest[1:-4]
    grad_context_ref, q_block, terms, sem = rest[-4:]
    g = group_of(meta, slot, swapped)
    depth = parts[0].shape[0]
    sums = {}
    for index, offset, wide, row_key, row_fn, col_fn in plan:
        start = pl.multiple_of(col_fn(meta) * wide, wide)
        term = lax.dot_general(
            grad_ref[:, pl.ds(start, wide)],
            parts[index][:, offset : offset + wide],
            NT_DIMS,
            preferred_element_type=F32,
        )
        sums[row_key] = (sums[row_key][0] + term if row_key in sums else term, row_fn)
    for total, row_fn in sums.values():
        grad_context_ref[row_fn(meta)] = total.astype(BF16)
    blocks = GROUP_WIDTH // depth
    grad_context = jnp.concatenate([grad_context_ref[b] for b in range(blocks)], axis=1)
    wide_start = pl.multiple_of(g * GROUP_WIDTH, GROUP_WIDTH)
    q_all = q_ref[:, pl.ds(wide_start, GROUP_WIDTH)]
    context_all = context_ref[:, pl.ds(wide_start, GROUP_WIDTH)]
    key_start = pl.multiple_of(g * HEAD_WIDTH, HEAD_WIDTH)
    value_start = pl.multiple_of(KEY_WIDTH + g * HEAD_WIDTH, HEAD_WIDTH)
    terms[...] = jnp.zeros_like(terms)
    for u in range(units):
        span = slice(u * rows, (u + 1) * rows)
        q_part = stack_heads(q_all[span])
        grad_part = stack_heads(grad_context[span])
        context_part = stack_heads(context_all[span])
        keys = windows_ref[u, :, pl.ds(key_start, HEAD_WIDTH)]
        values = windows_ref[u, :, pl.ds(value_start, HEAD_WIDTH)]
        probs = probs_ref[g, u]
        delta = jnp.sum(
            grad_part.astype(F32) * context_part.astype(F32), axis=1, keepdims=True
        )
        grad_probs = lax.dot_general(grad_part, values, NT_DIMS, preferred_element_type=F32)
        grad_scores = (probs * (grad_probs - delta) * SCALE).astype(BF16)
        q_part_grad = jnp.dot(grad_scores, keys, preferred_element_type=F32).astype(BF16)
        for h in range(RATIO):
            q_block[span, h * HEAD_WIDTH : (h + 1) * HEAD_WIDTH] = q_part_grad[
                h * rows : (h + 1) * rows
            ]
        key_term = lax.dot_general(grad_scores, q_part, TN_DIMS, preferred_element_type=F32)
        value_term = lax.dot_general(
            probs.astype(BF16), grad_part, TN_DIMS, preferred_element_type=F32
        )
        place = pl.ds(pl.multiple_of(meta[3 + units + u], rows), width)
        terms[place, :] += jnp.concatenate([key_term, value_term], axis=1)
    copy = pltpu.make_async_copy(q_block, q_grad_ref.at[:, pl.ds(wide_start, GROUP_WIDTH)], sem)
    copy.start()
    for t in range(groups):
        owner = jnp.bitwise_xor(meta[0], t)
        for u in range(units):
            shard = lax.rem(owner - meta[3 + u] + groups, groups)
            start = pl.multiple_of(shard * per_shard + u * rows, rows)
            share = terms[pl.ds(start, rows), :].astype(BF16)
            if stack:
                outs[0][owner, u * rows : (u + 1) * rows, :] = share
            else:
                outs[t][u * rows : (u + 1) * rows, :] = share
    copy.wait()


def project_kernel(slot, swapped, plan, first, meta, context_ref, *refs):
    count = 1 + max(entry[0] for entry in plan)
    parts = refs[:count]
    out_ref = refs[-1]
    total_ref = None if first else refs[count]
    g = group_of(meta, slot, swapped)
    by_columns = {}
    for index, offset, wide, row_key, row_fn, col_fn in plan:
        depth = parts[index].shape[0]
        start = pl.multiple_of(g * GROUP_WIDTH + row_fn(meta) * depth, depth)
        term = jnp.dot(
            context_ref[:, pl.ds(start, depth)],
            parts[index][:, offset : offset + wide],
            preferred_element_type=F32,
        )
        key = (id(col_fn), wide)
        if key in by_columns:
            by_columns[key] = (by_columns[key][0] + term, col_fn, wide)
        else:
            by_columns[key] = (term, col_fn, wide)
    for term, col_fn, wide in by_columns.values():
        span = pl.ds(pl.multiple_of(col_fn(meta) * wide, wide), wide)
        if not first:
            term = term + total_ref[:, span]
        out_ref[:, span] = term.astype(out_ref.dtype)


def combine_kernel(groups, order, swapped, with_out, meta, *refs):
    parts = refs[:groups]
    out_ref, sums, sems = refs[groups + with_out :]
    blocks = [part[...] for part in parts]
    if groups == 1:
        blocks = [parts[0][i] for i in range(parts[0].shape[0])]
    total = blocks[0].astype(F32)
    for block in blocks[1:]:
        total = total + block.astype(F32)
    sums[...] = total.astype(BF16)
    copies = []
    for index, slot in enumerate(order):
        g = group_of(meta, slot, swapped)
        for k in range(2):
            start = pl.multiple_of(k * KEY_WIDTH + g * HEAD_WIDTH, HEAD_WIDTH)
            copies.append(
                pltpu.make_async_copy(
                    sums.at[:, pl.ds((2 * index + k) * HEAD_WIDTH, HEAD_WIDTH)],
                    out_ref.at[:, pl.ds(start, HEAD_WIDTH)],
                    sems.at[2 * index + k],
                )
            )
    for copy in copies:
        copy.start()
    for copy in copies:
        copy.wait()


def zero_of(meta):
    return 0


def one_of(meta):
    return 1


def same_core(meta):
    return meta[2]


def other_core(meta):
    return 1 - meta[2]


def on_device(queries, keys_values, grad_out, out_proj, doc_lengths, tile_mask, unit_dest):
    groups = lax.axis_size("ctx")
    batches = lax.axis_size("dp")
    me = lax.axis_index("ctx").astype(jnp.int32)
    row = lax.axis_index("dp").astype(jnp.int32)
    per_shard = queries.shape[1]
    model = grad_out.shape[2]
    unit_count = unit_dest.shape[2]
    rows = per_shard // unit_count
    total_rows = per_shard * groups
    longest = total_rows // 8
    width = longest + rows
    lengths, tiles, routes = doc_lengths[0], tile_mask[0], unit_dest[0]
    offsets = routes[0]

    def move(block, fn):
        pairs = []
        for d in range(batches):
            for c in range(groups):
                d2, c2 = fn(d, c)
                pairs.append((d * groups + c, d2 * groups + c2))
        return lax.ppermute(block, ("dp", "ctx"), pairs)

    def to_ctx(block, t):
        return move(block, lambda d, c: (d, c ^ t))

    def to_core(block):
        return move(block, lambda d, c: (d ^ 1, c))

    def to_chip(block, j):
        return move(block, lambda d, c: (d ^ (2 * j), c))

    def after(block, *others):
        return lax.optimization_barrier((block,) + others)[0]

    swapped = (batches // 2) * GROUP_WIDTH == QUERY_HEADS * HEAD_WIDTH and groups == 4
    dests_meta = jnp.concatenate([jnp.stack([me, row // 2, lax.rem(row, 2)]), offsets])
    head_width = QUERY_HEADS * HEAD_WIDTH
    fold = head_width // (2 * KEY_WIDTH)
    sources = lax.rem(me - offsets + groups, groups)
    quarter = model // groups
    half = model // 2
    wide_far = quarter if swapped else 0
    shapes = [jax.ShapeDtypeStruct((per_shard + fold * rows, 2 * KEY_WIDTH), BF16)] * (groups - 1)
    if swapped:
        shapes.append(jax.ShapeDtypeStruct((out_proj.shape[0], quarter), BF16))
    sent = pl.pallas_call(
        functools.partial(pack_kernel, groups, unit_count, rows, fold, wide_far),
        out_shape=tuple(shapes),
        in_specs=[in_smem(), anywhere(), anywhere()] + [anywhere()] * int(swapped),
        out_specs=(whole(),) * len(shapes),
        scratch_shapes=[pltpu.SemaphoreType.DMA(((groups - 1) * (1 + fold) + int(swapped),))],
        name="pack",
    )(unit_dest, queries[0], keys_values[0], *([out_proj] if swapped else []))
    if swapped:
        two = to_chip(sent[-1], 2)
        sent = sent[:-1]
    sent = list(sent)
    if swapped:
        own_other = to_core(out_proj)
        one_a = to_chip(after(out_proj[:, :half], own_other), 1)
        sent[-1] = after(sent[-1], own_other)
    kv_parts = [keys_values[0]] + [to_ctx(sent[t - 1], t) for t in range(1, groups)]

    unit_ids = jnp.arange(unit_count, dtype=jnp.int32)
    first_pos = sources * per_shard + unit_ids * rows
    query_pos = first_pos[:, None] + jnp.arange(rows, dtype=jnp.int32)[None, :]
    win_start = jnp.clip(first_pos - longest, 0, total_rows - width)
    key_pos = win_start[:, None] + jnp.arange(width, dtype=jnp.int32)[None, :]
    allowed = window_mask(query_pos, key_pos, lengths, tiles).astype(F32)
    meta = jnp.concatenate([dests_meta, win_start]).astype(jnp.int32)

    params = pltpu.CompilerParams(vmem_limit_bytes=(16 if swapped else 40) * MIB)
    sizes = (groups, unit_count, rows, width, per_shard)
    stacked = RATIO * rows
    context, probs, windows, my_queries = pl.pallas_call(
        functools.partial(forward_kernel, *sizes, fold),
        out_shape=(
            jax.ShapeDtypeStruct((per_shard, QUERY_HEADS * HEAD_WIDTH), BF16),
            jax.ShapeDtypeStruct((KEY_VALUE_HEADS, unit_count, stacked, width), F32),
            jax.ShapeDtypeStruct((unit_count, width, 2 * KEY_WIDTH), BF16),
            jax.ShapeDtypeStruct((per_shard, head_width), BF16),
        ),
        in_specs=[in_smem(), whole(), anywhere()] + [anywhere()] * groups,
        out_specs=(whole(),) * 4,
        scratch_shapes=[
            pltpu.VMEM((total_rows, 2 * KEY_WIDTH), BF16),
            pltpu.SemaphoreType.DMA((groups,)),
            pltpu.SemaphoreType.DMA((unit_count, fold)),
        ],
        compiler_params=params,
        cost_estimate=pl.CostEstimate(
            flops=4 * unit_count * QUERY_HEADS * rows * width * HEAD_WIDTH * 8,
            bytes_accessed=8 * 1024 * 1024,
            transcendentals=unit_count * QUERY_HEADS * rows * width,
        ),
        name="forward",
    )(meta, allowed, queries[0], *kv_parts)

    q_grad = None
    total = None

    def arrange(parts):
        arrays, plan = [], []
        for block, offset, wide, *entry in parts:
            found = [i for i, array in enumerate(arrays) if array is block]
            if not found:
                arrays.append(block)
            plan.append((found[0] if found else len(arrays) - 1, offset, wide, *entry))
        return arrays, plan

    def grad_step(slot, parts, q_grad, stack=False):
        arrays, plan = arrange(parts)
        depth = arrays[0].shape[0]
        with_q = q_grad is not None
        results = pl.pallas_call(
            functools.partial(grad_kernel, *sizes, slot, swapped, plan, with_q, stack),
            out_shape=(jax.ShapeDtypeStruct((per_shard, QUERY_HEADS * HEAD_WIDTH), BF16),)
            + (
                (jax.ShapeDtypeStruct((groups, per_shard, 2 * HEAD_WIDTH), BF16),)
                if stack
                else (jax.ShapeDtypeStruct((per_shard, 2 * HEAD_WIDTH), BF16),) * groups
            ),
            in_specs=[in_smem()]
            + [whole()] * (5 + len(arrays))
            + ([anywhere()] if with_q else []),
            out_specs=(anywhere(),) + (whole(),) * (1 if stack else groups),
            scratch_shapes=[
                pltpu.VMEM((GROUP_WIDTH // depth, per_shard, depth), BF16),
                pltpu.VMEM((per_shard, GROUP_WIDTH), BF16),
                pltpu.VMEM((total_rows, 2 * HEAD_WIDTH), F32),
                pltpu.SemaphoreType.DMA,
            ],
            input_output_aliases={6 + len(arrays): 0} if with_q else {},
            compiler_params=params,
            cost_estimate=pl.CostEstimate(
                flops=2 * per_shard * GROUP_WIDTH * model * 2,
                bytes_accessed=3 * GROUP_WIDTH * model * 2,
                transcendentals=0,
            ),
            name=f"grad_{slot}",
        )(
            meta, grad_out[0], my_queries, context, probs, windows, *arrays,
            *([q_grad] if with_q else []),
        )
        return results[0], results[1:]

    def send_shares(mine):
        return [mine[0]] + [to_ctx(mine[t], t) for t in range(1, groups)]

    def project_step(slot, parts, total, last):
        arrays, plan = arrange(parts)
        first = total is None
        return pl.pallas_call(
            functools.partial(project_kernel, slot, swapped, plan, first),
            out_shape=jax.ShapeDtypeStruct((per_shard, model), BF16 if last else F32),
            in_specs=[in_smem()] + [whole()] * (1 + len(arrays) + (0 if first else 1)),
            out_specs=whole(),
            compiler_params=params,
            cost_estimate=pl.CostEstimate(
                flops=2 * per_shard * GROUP_WIDTH * model,
                bytes_accessed=2 * GROUP_WIDTH * model * 2,
                transcendentals=0,
            ),
            name=f"project_{slot}",
        )(meta, context, *arrays, *([] if first else [total]))

    count = KEY_VALUE_HEADS
    if swapped:
        order = (0, 2, 1, 3)
        columns = [
            functools.partial(lambda t, meta: jnp.bitwise_xor(meta[0], t), t)
            for t in range(groups)
        ]

        def own(block, column, offset=0, wide=None):
            return (block, offset, wide or block.shape[1], "own", same_core, column)

        def other(block, column, offset=0, wide=None):
            return (block, offset, wide or block.shape[1], "other", other_core, column)

        three = to_chip(two, 1)
        parts_0 = [own(out_proj, zero_of), other(own_other, zero_of)]
        q_grad, mine_0 = grad_step(0, parts_0, None)
        total = project_step(0, parts_0, None, False)
        twos = [two] + [to_ctx(after(two, *kv_parts[1:]), t) for t in range(1, groups)]
        one_b = to_chip(after(out_proj[:, half:], one_a), 1)
        middle = to_core(jnp.concatenate([one_a, three] + twos[:3] + [after(twos[3], total, mine_0[0])], axis=1))
        parts_2 = [own(twos[t], columns[t]) for t in range(groups)]
        parts_2 += [other(middle, columns[t], half + quarter + t * quarter, quarter) for t in range(groups)]
        threes = [three] + [to_ctx(after(three, *twos[1:]), t) for t in range(1, groups)]
        q_grad, mine_2 = grad_step(2, parts_2, q_grad)
        total = project_step(2, parts_2, total, False)
        one_b_other = to_core(after(one_b, total, mine_2[0], *threes[1:]))
        parts_1 = [
            own(one_a, zero_of),
            other(middle, zero_of, 0, half),
            own(one_b, one_of),
            other(one_b_other, one_of),
        ]
        parts_3 = [
            own(three, columns[0]),
            other(middle, columns[0], half, quarter),
        ]
        for t in range(1, groups):
            parts_3 += [own(threes[t], columns[t]), other(to_core(threes[t]), columns[t])]
        q_grad, mine_1 = grad_step(1, parts_1, q_grad)
        q_grad, mine_3 = grad_step(3, parts_3, q_grad)
        early = send_shares(
            [jnp.concatenate([mine_0[t], mine_2[t], mine_1[t]], axis=1) for t in range(groups)]
        )
        late = send_shares(mine_3)
        total = project_step(1, parts_1, total, False)
        total = project_step(3, parts_3, total, True)
        batches_of_shares = [((0, 2, 1), early), ((3,), late)]
    else:
        full = lax.all_gather(out_proj, "dp", axis=0, tiled=True)
        batches_of_shares = []
        for g in range(count):
            part = full[g * GROUP_WIDTH : (g + 1) * GROUP_WIDTH]
            parts = [(part, 0, model, "own", zero_of, zero_of)]
            q_grad, mine = grad_step(g, parts, q_grad)
            batches_of_shares.append(((g,), send_shares(mine)))
            total = project_step(g, parts, total, g == count - 1)

    kv_grad = None
    for order, share in batches_of_shares:
        with_out = kv_grad is not None
        kv_grad = pl.pallas_call(
            functools.partial(combine_kernel, len(share), order, swapped, int(with_out)),
            out_shape=jax.ShapeDtypeStruct((per_shard, 2 * KEY_WIDTH), BF16),
            in_specs=[in_smem()] + [whole()] * len(share) + [anywhere()] * int(with_out),
            out_specs=anywhere(),
            scratch_shapes=[
                pltpu.VMEM((per_shard, 2 * HEAD_WIDTH * len(order)), BF16),
                pltpu.SemaphoreType.DMA((2 * len(order),)),
            ],
            input_output_aliases={1 + len(share): 0} if with_out else {},
            compiler_params=params,
            name=f"combine_{order[0]}",
        )(meta, *share, *([kv_grad] if with_out else []))
    return (total[None], q_grad[None], kv_grad[None])


def solution(mesh):
    return jax.shard_map(
        on_device,
        mesh=mesh,
        in_specs=(
            P("dp", "ctx", None),
            P("dp", "ctx", None),
            P("dp", "ctx", None),
            P("dp", None),
            P("dp", None),
            P("dp", None, None),
            P("dp", None, None),
        ),
        out_specs=(P("dp", "ctx", None), P("dp", "ctx", None), P("dp", "ctx", None)),
        check_vma=False,
    )
```

```python
import functools
import math

import jax
import jax.numpy as jnp
from jax import lax
from jax.experimental import pallas as pl
from jax.experimental.pallas import tpu as pltpu
from jax.sharding import PartitionSpec as P

QUERY_HEADS = 16
KEY_VALUE_HEADS = 4
HEAD_WIDTH = 128
TILE = 128
RATIO = QUERY_HEADS // KEY_VALUE_HEADS
GROUP_WIDTH = RATIO * HEAD_WIDTH
KEY_WIDTH = KEY_VALUE_HEADS * HEAD_WIDTH
SCALE = 1.0 / math.sqrt(HEAD_WIDTH)
F32 = jnp.float32
BF16 = jnp.bfloat16
NT_DIMS = (((1,), (1,)), ((), ()))
TN_DIMS = (((0,), (0,)), ((), ()))
MIB = 1024 * 1024


def whole():
    return pl.BlockSpec(memory_space=pltpu.VMEM)


def in_smem():
    return pl.BlockSpec(memory_space=pltpu.SMEM)


def anywhere():
    return pl.BlockSpec(memory_space=pl.ANY)


def dialogue_of(positions, lengths):
    bounds = jnp.cumsum(lengths)[:-1]
    return jnp.sum((positions[:, None] >= bounds[None, :]).astype(jnp.int32), axis=1)


def window_mask(query_pos, key_pos, lengths, tiles):
    query_doc = dialogue_of(query_pos.reshape(-1), lengths).reshape(query_pos.shape)
    key_doc = dialogue_of(key_pos.reshape(-1), lengths).reshape(key_pos.shape)
    tile_ids = jnp.arange(tiles.shape[0], dtype=jnp.int32)
    query_tiles = (query_pos[:, :, None] // TILE == tile_ids[None, None, :]).astype(F32)
    key_tiles = (key_pos[:, :, None] // TILE == tile_ids[None, None, :]).astype(F32)
    tile_rows = jnp.einsum("ucn,nm->ucm", query_tiles, tiles.astype(F32))
    tile_open = jnp.einsum("ucm,uwm->ucw", tile_rows, key_tiles) > 0.5
    same_doc = query_doc[:, :, None] == key_doc[:, None, :]
    causal = key_pos[:, None, :] <= query_pos[:, :, None]
    return tile_open & same_doc & causal


def stack_heads(block):
    return jnp.concatenate(
        [block[:, h * HEAD_WIDTH : (h + 1) * HEAD_WIDTH] for h in range(RATIO)], axis=0
    )


def pack_kernel(groups, units, rows, fold, wide_far, routes, q_ref, kv_ref, *refs):
    outs, sems = refs[:-1], refs[-1]
    per_shard, wide = kv_ref.shape
    me = lax.axis_index("ctx")
    copies = []
    if wide_far:
        block_ref, outs = outs[0], outs[1:]
        start = pl.multiple_of(me * wide_far, wide_far)
        copies.append((block_ref.at[:, pl.ds(start, wide_far)], outs[-1]))
    for t in range(1, groups):
        chosen = 0
        for j in range(units):
            dest = lax.rem(me + routes[0, 0, j], groups)
            chosen = chosen + jnp.where(dest == jnp.bitwise_xor(me, t), j, 0)
        start = pl.multiple_of(chosen * rows, rows)
        copies.append((kv_ref, outs[t - 1].at[pl.ds(0, per_shard)]))
        for f in range(fold):
            copies.append(
                (
                    q_ref.at[pl.ds(start, rows), pl.ds(f * wide, wide)],
                    outs[t - 1].at[pl.ds(per_shard + f * rows, rows)],
                )
            )
    copies = [
        pltpu.make_async_copy(source, target, sems.at[i])
        for i, (source, target) in enumerate(copies)
    ]
    for copy in copies:
        copy.start()
    for copy in copies:
        copy.wait()


def forward_kernel(groups, units, rows, width, per_shard, fold, *refs):
    meta, allowed_ref, own_q = refs[:3]
    kv_parts = refs[3 : 3 + groups]
    context_ref, probs_ref, windows_ref, q_ref = refs[3 + groups : 7 + groups]
    kv_ref, kv_sems, q_sems = refs[7 + groups :]
    me = meta[0]
    wide = kv_ref.shape[1]
    for t in range(groups):
        start = pl.multiple_of(jnp.bitwise_xor(me, t) * per_shard, per_shard)
        pltpu.make_async_copy(
            kv_parts[t].at[pl.ds(0, per_shard)], kv_ref.at[pl.ds(start, per_shard)], kv_sems.at[t]
        ).start()
    for u in range(units):
        source = lax.rem(me - meta[3 + u] + groups, groups)
        for t in range(groups):

            @pl.when(source == jnp.bitwise_xor(me, t))
            def _():
                for f in range(fold):
                    if t == 0:
                        part = own_q.at[pl.ds(u * rows, rows), pl.ds(f * wide, wide)]
                    else:
                        part = kv_parts[t].at[pl.ds(per_shard + f * rows, rows)]
                    pltpu.make_async_copy(
                        part,
                        q_ref.at[pl.ds(u * rows, rows), pl.ds(f * wide, wide)],
                        q_sems.at[u, f],
                    ).start()

    for t in range(groups):
        start = pl.multiple_of(jnp.bitwise_xor(me, t) * per_shard, per_shard)
        pltpu.make_async_copy(
            kv_parts[t].at[pl.ds(0, per_shard)], kv_ref.at[pl.ds(start, per_shard)], kv_sems.at[t]
        ).wait()
    for u in range(units):
        for f in range(fold):
            pltpu.make_async_copy(
                own_q.at[pl.ds(u * rows, rows), pl.ds(f * wide, wide)],
                q_ref.at[pl.ds(u * rows, rows), pl.ds(f * wide, wide)],
                q_sems.at[u, f],
            ).wait()
    for u in range(units):
        start = pl.multiple_of(meta[3 + units + u], rows)
        window = kv_ref[pl.ds(start, width), :]
        windows_ref[u] = window
        mask = jnp.concatenate([allowed_ref[u]] * RATIO, axis=0) > 0.5
        for g in range(KEY_VALUE_HEADS):
            q_part = stack_heads(
                q_ref[u * rows : (u + 1) * rows, g * GROUP_WIDTH : (g + 1) * GROUP_WIDTH]
            )
            keys = window[:, g * HEAD_WIDTH : (g + 1) * HEAD_WIDTH]
            values = window[:, KEY_WIDTH + g * HEAD_WIDTH : KEY_WIDTH + (g + 1) * HEAD_WIDTH]
            raw = lax.dot_general(q_part, keys, NT_DIMS, preferred_element_type=F32) * SCALE
            masked = jnp.where(mask, raw, -1e30)
            top = jnp.max(masked, axis=1, keepdims=True)
            expo = jnp.exp(masked - top)
            probs = expo / jnp.sum(expo, axis=1, keepdims=True)
            probs_ref[g, u] = probs
            mixed = jnp.dot(probs.astype(BF16), values, preferred_element_type=F32).astype(BF16)
            for h in range(RATIO):
                col = (g * RATIO + h) * HEAD_WIDTH
                context_ref[u * rows : (u + 1) * rows, col : col + HEAD_WIDTH] = mixed[
                    h * rows : (h + 1) * rows
                ]


def group_of(meta, slot, swapped):
    return jnp.bitwise_xor(meta[1], slot) if swapped else slot


def grad_kernel(groups, units, rows, width, per_shard, slot, swapped, plan, with_q, stack, *refs):
    meta, grad_ref, q_ref, context_ref, probs_ref, windows_ref = refs[:6]
    count = 1 + max(entry[0] for entry in plan)
    parts = refs[6 : 6 + count]
    rest = refs[6 + count :]
    if with_q:
        rest = rest[1:]
    q_grad_ref = rest[0]
    outs = rest[1:-4]
    grad_context_ref, q_block, terms, sem = rest[-4:]
    g = group_of(meta, slot, swapped)
    depth = parts[0].shape[0]
    sums = {}
    for index, offset, wide, row_key, row_fn, col_fn in plan:
        start = pl.multiple_of(col_fn(meta) * wide, wide)
        term = lax.dot_general(
            grad_ref[:, pl.ds(start, wide)],
            parts[index][:, offset : offset + wide],
            NT_DIMS,
            preferred_element_type=F32,
        )
        sums[row_key] = (sums[row_key][0] + term if row_key in sums else term, row_fn)
    for total, row_fn in sums.values():
        grad_context_ref[row_fn(meta)] = total.astype(BF16)
    blocks = GROUP_WIDTH // depth
    grad_context = jnp.concatenate([grad_context_ref[b] for b in range(blocks)], axis=1)
    wide_start = pl.multiple_of(g * GROUP_WIDTH, GROUP_WIDTH)
    q_all = q_ref[:, pl.ds(wide_start, GROUP_WIDTH)]
    context_all = context_ref[:, pl.ds(wide_start, GROUP_WIDTH)]
    key_start = pl.multiple_of(g * HEAD_WIDTH, HEAD_WIDTH)
    value_start = pl.multiple_of(KEY_WIDTH + g * HEAD_WIDTH, HEAD_WIDTH)
    terms[...] = jnp.zeros_like(terms)
    for u in range(units):
        span = slice(u * rows, (u + 1) * rows)
        q_part = stack_heads(q_all[span])
        grad_part = stack_heads(grad_context[span])
        context_part = stack_heads(context_all[span])
        keys = windows_ref[u, :, pl.ds(key_start, HEAD_WIDTH)]
        values = windows_ref[u, :, pl.ds(value_start, HEAD_WIDTH)]
        probs = probs_ref[g, u]
        delta = jnp.sum(
            grad_part.astype(F32) * context_part.astype(F32), axis=1, keepdims=True
        )
        grad_probs = lax.dot_general(grad_part, values, NT_DIMS, preferred_element_type=F32)
        grad_scores = (probs * (grad_probs - delta) * SCALE).astype(BF16)
        q_part_grad = jnp.dot(grad_scores, keys, preferred_element_type=F32).astype(BF16)
        for h in range(RATIO):
            q_block[span, h * HEAD_WIDTH : (h + 1) * HEAD_WIDTH] = q_part_grad[
                h * rows : (h + 1) * rows
            ]
        key_term = lax.dot_general(grad_scores, q_part, TN_DIMS, preferred_element_type=F32)
        value_term = lax.dot_general(
            probs.astype(BF16), grad_part, TN_DIMS, preferred_element_type=F32
        )
        place = pl.ds(pl.multiple_of(meta[3 + units + u], rows), width)
        terms[place, :] += jnp.concatenate([key_term, value_term], axis=1)
    copy = pltpu.make_async_copy(q_block, q_grad_ref.at[:, pl.ds(wide_start, GROUP_WIDTH)], sem)
    copy.start()
    for t in range(groups):
        owner = jnp.bitwise_xor(meta[0], t)
        for u in range(units):
            shard = lax.rem(owner - meta[3 + u] + groups, groups)
            start = pl.multiple_of(shard * per_shard + u * rows, rows)
            share = terms[pl.ds(start, rows), :].astype(BF16)
            if stack:
                outs[0][owner, u * rows : (u + 1) * rows, :] = share
            else:
                outs[t][u * rows : (u + 1) * rows, :] = share
    copy.wait()


def project_kernel(slot, swapped, plan, first, meta, context_ref, *refs):
    count = 1 + max(entry[0] for entry in plan)
    parts = refs[:count]
    out_ref = refs[-1]
    total_ref = None if first else refs[count]
    g = group_of(meta, slot, swapped)
    by_columns = {}
    for index, offset, wide, row_key, row_fn, col_fn in plan:
        depth = parts[index].shape[0]
        start = pl.multiple_of(g * GROUP_WIDTH + row_fn(meta) * depth, depth)
        term = jnp.dot(
            context_ref[:, pl.ds(start, depth)],
            parts[index][:, offset : offset + wide],
            preferred_element_type=F32,
        )
        key = (id(col_fn), wide)
        if key in by_columns:
            by_columns[key] = (by_columns[key][0] + term, col_fn, wide)
        else:
            by_columns[key] = (term, col_fn, wide)
    for term, col_fn, wide in by_columns.values():
        span = pl.ds(pl.multiple_of(col_fn(meta) * wide, wide), wide)
        if not first:
            term = term + total_ref[:, span]
        out_ref[:, span] = term.astype(out_ref.dtype)


def combine_kernel(groups, order, swapped, with_out, meta, *refs):
    parts = refs[:groups]
    out_ref, sums, sems = refs[groups + with_out :]
    blocks = [part[...] for part in parts]
    if groups == 1:
        blocks = [parts[0][i] for i in range(parts[0].shape[0])]
    total = blocks[0].astype(F32)
    for block in blocks[1:]:
        total = total + block.astype(F32)
    sums[...] = total.astype(BF16)
    copies = []
    for index, slot in enumerate(order):
        g = group_of(meta, slot, swapped)
        for k in range(2):
            start = pl.multiple_of(k * KEY_WIDTH + g * HEAD_WIDTH, HEAD_WIDTH)
            copies.append(
                pltpu.make_async_copy(
                    sums.at[:, pl.ds((2 * index + k) * HEAD_WIDTH, HEAD_WIDTH)],
                    out_ref.at[:, pl.ds(start, HEAD_WIDTH)],
                    sems.at[2 * index + k],
                )
            )
    for copy in copies:
        copy.start()
    for copy in copies:
        copy.wait()


def zero_of(meta):
    return 0


def one_of(meta):
    return 1


def same_core(meta):
    return meta[2]


def other_core(meta):
    return 1 - meta[2]


def on_device(queries, keys_values, grad_out, out_proj, doc_lengths, tile_mask, unit_dest):
    groups = lax.axis_size("ctx")
    batches = lax.axis_size("dp")
    me = lax.axis_index("ctx").astype(jnp.int32)
    row = lax.axis_index("dp").astype(jnp.int32)
    per_shard = queries.shape[1]
    model = grad_out.shape[2]
    unit_count = unit_dest.shape[2]
    rows = per_shard // unit_count
    total_rows = per_shard * groups
    longest = total_rows // 8
    width = longest + rows
    lengths, tiles, routes = doc_lengths[0], tile_mask[0], unit_dest[0]
    offsets = routes[0]

    def move(block, fn):
        pairs = []
        for d in range(batches):
            for c in range(groups):
                d2, c2 = fn(d, c)
                pairs.append((d * groups + c, d2 * groups + c2))
        return lax.ppermute(block, ("dp", "ctx"), pairs)

    def to_ctx(block, t):
        return move(block, lambda d, c: (d, c ^ t))

    def to_core(block):
        return move(block, lambda d, c: (d ^ 1, c))

    def to_chip(block, j):
        return move(block, lambda d, c: (d ^ (2 * j), c))

    def after(block, *others):
        return lax.optimization_barrier((block,) + others)[0]

    swapped = (batches // 2) * GROUP_WIDTH == QUERY_HEADS * HEAD_WIDTH and groups == 4
    dests_meta = jnp.concatenate([jnp.stack([me, row // 2, lax.rem(row, 2)]), offsets])
    head_width = QUERY_HEADS * HEAD_WIDTH
    fold = head_width // (2 * KEY_WIDTH)
    sources = lax.rem(me - offsets + groups, groups)
    quarter = model // groups
    half = model // 2
    wide_far = quarter if swapped else 0
    shapes = [jax.ShapeDtypeStruct((per_shard + fold * rows, 2 * KEY_WIDTH), BF16)] * (groups - 1)
    if swapped:
        shapes.append(jax.ShapeDtypeStruct((out_proj.shape[0], quarter), BF16))
    sent = pl.pallas_call(
        functools.partial(pack_kernel, groups, unit_count, rows, fold, wide_far),
        out_shape=tuple(shapes),
        in_specs=[in_smem(), anywhere(), anywhere()] + [anywhere()] * int(swapped),
        out_specs=(whole(),) * len(shapes),
        scratch_shapes=[pltpu.SemaphoreType.DMA(((groups - 1) * (1 + fold) + int(swapped),))],
        name="pack",
    )(unit_dest, queries[0], keys_values[0], *([out_proj] if swapped else []))
    if swapped:
        two = to_chip(sent[-1], 2)
        sent = sent[:-1]
    sent = list(sent)
    if swapped:
        own_other = to_core(out_proj)
        one_a = to_chip(after(out_proj[:, :half], own_other), 1)
        sent[-1] = after(sent[-1], own_other)
    kv_parts = [keys_values[0]] + [to_ctx(sent[t - 1], t) for t in range(1, groups)]

    unit_ids = jnp.arange(unit_count, dtype=jnp.int32)
    first_pos = sources * per_shard + unit_ids * rows
    query_pos = first_pos[:, None] + jnp.arange(rows, dtype=jnp.int32)[None, :]
    win_start = jnp.clip(first_pos - longest, 0, total_rows - width)
    key_pos = win_start[:, None] + jnp.arange(width, dtype=jnp.int32)[None, :]
    allowed = window_mask(query_pos, key_pos, lengths, tiles).astype(F32)
    meta = jnp.concatenate([dests_meta, win_start]).astype(jnp.int32)

    params = pltpu.CompilerParams(vmem_limit_bytes=(16 if swapped else 40) * MIB)
    sizes = (groups, unit_count, rows, width, per_shard)
    stacked = RATIO * rows
    context, probs, windows, my_queries = pl.pallas_call(
        functools.partial(forward_kernel, *sizes, fold),
        out_shape=(
            jax.ShapeDtypeStruct((per_shard, QUERY_HEADS * HEAD_WIDTH), BF16),
            jax.ShapeDtypeStruct((KEY_VALUE_HEADS, unit_count, stacked, width), F32),
            jax.ShapeDtypeStruct((unit_count, width, 2 * KEY_WIDTH), BF16),
            jax.ShapeDtypeStruct((per_shard, head_width), BF16),
        ),
        in_specs=[in_smem(), whole(), anywhere()] + [anywhere()] * groups,
        out_specs=(whole(),) * 4,
        scratch_shapes=[
            pltpu.VMEM((total_rows, 2 * KEY_WIDTH), BF16),
            pltpu.SemaphoreType.DMA((groups,)),
            pltpu.SemaphoreType.DMA((unit_count, fold)),
        ],
        compiler_params=params,
        cost_estimate=pl.CostEstimate(
            flops=4 * unit_count * QUERY_HEADS * rows * width * HEAD_WIDTH * 8,
            bytes_accessed=8 * 1024 * 1024,
            transcendentals=unit_count * QUERY_HEADS * rows * width,
        ),
        name="forward",
    )(meta, allowed, queries[0], *kv_parts)

    q_grad = None
    total = None

    def arrange(parts):
        arrays, plan = [], []
        for block, offset, wide, *entry in parts:
            found = [i for i, array in enumerate(arrays) if array is block]
            if not found:
                arrays.append(block)
            plan.append((found[0] if found else len(arrays) - 1, offset, wide, *entry))
        return arrays, plan

    def grad_step(slot, parts, q_grad, stack=False):
        arrays, plan = arrange(parts)
        depth = arrays[0].shape[0]
        with_q = q_grad is not None
        results = pl.pallas_call(
            functools.partial(grad_kernel, *sizes, slot, swapped, plan, with_q, stack),
            out_shape=(jax.ShapeDtypeStruct((per_shard, QUERY_HEADS * HEAD_WIDTH), BF16),)
            + (
                (jax.ShapeDtypeStruct((groups, per_shard, 2 * HEAD_WIDTH), BF16),)
                if stack
                else (jax.ShapeDtypeStruct((per_shard, 2 * HEAD_WIDTH), BF16),) * groups
            ),
            in_specs=[in_smem()]
            + [whole()] * (5 + len(arrays))
            + ([anywhere()] if with_q else []),
            out_specs=(anywhere(),) + (whole(),) * (1 if stack else groups),
            scratch_shapes=[
                pltpu.VMEM((GROUP_WIDTH // depth, per_shard, depth), BF16),
                pltpu.VMEM((per_shard, GROUP_WIDTH), BF16),
                pltpu.VMEM((total_rows, 2 * HEAD_WIDTH), F32),
                pltpu.SemaphoreType.DMA,
            ],
            input_output_aliases={6 + len(arrays): 0} if with_q else {},
            compiler_params=params,
            cost_estimate=pl.CostEstimate(
                flops=2 * per_shard * GROUP_WIDTH * model * 2,
                bytes_accessed=3 * GROUP_WIDTH * model * 2,
                transcendentals=0,
            ),
            name=f"grad_{slot}",
        )(
            meta, grad_out[0], my_queries, context, probs, windows, *arrays,
            *([q_grad] if with_q else []),
        )
        return results[0], results[1:]

    def send_shares(mine):
        return [mine[0]] + [to_ctx(mine[t], t) for t in range(1, groups)]

    def project_step(slot, parts, total, last):
        arrays, plan = arrange(parts)
        first = total is None
        return pl.pallas_call(
            functools.partial(project_kernel, slot, swapped, plan, first),
            out_shape=jax.ShapeDtypeStruct((per_shard, model), BF16 if last else F32),
            in_specs=[in_smem()] + [whole()] * (1 + len(arrays) + (0 if first else 1)),
            out_specs=whole(),
            compiler_params=params,
            cost_estimate=pl.CostEstimate(
                flops=2 * per_shard * GROUP_WIDTH * model,
                bytes_accessed=2 * GROUP_WIDTH * model * 2,
                transcendentals=0,
            ),
            name=f"project_{slot}",
        )(meta, context, *arrays, *([] if first else [total]))

    count = KEY_VALUE_HEADS
    if swapped:
        order = (0, 2, 1, 3)
        columns = [
            functools.partial(lambda t, meta: jnp.bitwise_xor(meta[0], t), t)
            for t in range(groups)
        ]

        def own(block, column, offset=0, wide=None):
            return (block, offset, wide or block.shape[1], "own", same_core, column)

        def other(block, column, offset=0, wide=None):
            return (block, offset, wide or block.shape[1], "other", other_core, column)

        three = to_chip(two, 1)
        parts_0 = [own(out_proj, zero_of), other(own_other, zero_of)]
        q_grad, mine_0 = grad_step(0, parts_0, None)
        total = project_step(0, parts_0, None, False)
        twos = [two] + [to_ctx(after(two, *kv_parts[1:]), t) for t in range(1, groups)]
        one_b = to_chip(after(out_proj[:, half:], one_a), 1)
        middle = to_core(jnp.concatenate([one_a, three] + twos[:3] + [after(twos[3], total, mine_0[0])], axis=1))
        parts_2 = [own(twos[t], columns[t]) for t in range(groups)]
        parts_2 += [other(middle, columns[t], half + quarter + t * quarter, quarter) for t in range(groups)]
        threes = [three] + [to_ctx(after(three, *twos[1:3]), t) for t in range(1, groups)]
        q_grad, mine_2 = grad_step(2, parts_2, q_grad)
        total = project_step(2, parts_2, total, False)
        one_b_other = to_core(after(one_b, total, mine_2[0], *threes[1:]))
        parts_1 = [
            own(one_a, zero_of),
            other(middle, zero_of, 0, half),
            own(one_b, one_of),
            other(one_b_other, one_of),
        ]
        parts_3 = [
            own(three, columns[0]),
            other(middle, columns[0], half, quarter),
        ]
        for t in range(1, groups):
            parts_3 += [own(threes[t], columns[t]), other(to_core(threes[t]), columns[t])]
        q_grad, mine_1 = grad_step(1, parts_1, q_grad)
        q_grad, mine_3 = grad_step(3, parts_3, q_grad)
        early = send_shares(
            [jnp.concatenate([mine_0[t], mine_2[t], mine_1[t]], axis=1) for t in range(groups)]
        )
        late = send_shares(mine_3)
        total = project_step(1, parts_1, total, False)
        total = project_step(3, parts_3, total, True)
        batches_of_shares = [((0, 2, 1), early), ((3,), late)]
    else:
        full = lax.all_gather(out_proj, "dp", axis=0, tiled=True)
        batches_of_shares = []
        for g in range(count):
            part = full[g * GROUP_WIDTH : (g + 1) * GROUP_WIDTH]
            parts = [(part, 0, model, "own", zero_of, zero_of)]
            q_grad, mine = grad_step(g, parts, q_grad)
            batches_of_shares.append(((g,), send_shares(mine)))
            total = project_step(g, parts, total, g == count - 1)

    kv_grad = None
    for order, share in batches_of_shares:
        with_out = kv_grad is not None
        kv_grad = pl.pallas_call(
            functools.partial(combine_kernel, len(share), order, swapped, int(with_out)),
            out_shape=jax.ShapeDtypeStruct((per_shard, 2 * KEY_WIDTH), BF16),
            in_specs=[in_smem()] + [whole()] * len(share) + [anywhere()] * int(with_out),
            out_specs=anywhere(),
            scratch_shapes=[
                pltpu.VMEM((per_shard, 2 * HEAD_WIDTH * len(order)), BF16),
                pltpu.SemaphoreType.DMA((2 * len(order),)),
            ],
            input_output_aliases={1 + len(share): 0} if with_out else {},
            compiler_params=params,
            name=f"combine_{order[0]}",
        )(meta, *share, *([kv_grad] if with_out else []))
    return (total[None], q_grad[None], kv_grad[None])


def solution(mesh):
    return jax.shard_map(
        on_device,
        mesh=mesh,
        in_specs=(
            P("dp", "ctx", None),
            P("dp", "ctx", None),
            P("dp", "ctx", None),
            P("dp", None),
            P("dp", None),
            P("dp", None, None),
            P("dp", None, None),
        ),
        out_specs=(P("dp", "ctx", None), P("dp", "ctx", None), P("dp", "ctx", None)),
        check_vma=False,
    )
```
